32 devices in a mesh: dp: 4 (over z), seq: 2 (over x), mp: 4 (over y, core).
Axes of the slice: x: 2, y: 2, z: 4, core: 2. Of those that a mesh axis runs over, the one named last changes fastest.
Arguments:
- inputs: bfloat16 [2048, 1536], P(('dp', 'seq')), may hold values from -6 to 6
- cotangent: bfloat16 [2048, 1536], P(('dp', 'seq')), may hold values from -6 to 6
- segments: int32 [2048], P('dp'), may hold values from 0 to 4, as said below
- positions: int32 [2048], P(('dp', 'seq')), may hold values from 0 to 255, as said below
- w_query: bfloat16 [1536, 1536], P(('dp', 'seq'), 'mp'), may hold values from -0.15625 to 0.15625
- w_key: bfloat16 [1536, 256], P(('dp', 'seq', 'mp')), may hold values from -0.15625 to 0.15625
- w_value: bfloat16 [1536, 256], P(('dp', 'seq', 'mp')), may hold values from -0.15625 to 0.15625
- bias_query: bfloat16 [1536], P(('dp', 'seq', 'mp')), may hold values from -1.5 to 1.5
- bias_key: bfloat16 [256], P(('dp', 'seq', 'mp')), may hold values from -3 to 3
- bias_value: bfloat16 [256], P(('dp', 'seq', 'mp')), may hold values from -3 to 3
- w_out: bfloat16 [1536, 1536], P('mp', ('dp', 'seq')), may hold values from -1 to 1
- gain_attn: bfloat16 [1536], P(('dp', 'seq', 'mp')), may hold values from 0.5 to 1.5
- gain_ffn: bfloat16 [1536], P(('dp', 'seq', 'mp')), may hold values from 0.5 to 1.5
- w_gate: bfloat16 [1536, 8960], P(('dp', 'seq'), 'mp'), may hold values from -0.15625 to 0.15625
- w_up: bfloat16 [1536, 8960], P(('dp', 'seq'), 'mp'), may hold values from -0.15625 to 0.15625
- w_down: bfloat16 [8960, 1536], P('mp', ('dp', 'seq')), may hold values from -0.5 to 0.5
Outputs:
- output: float32 [2048, 1536], P(('dp', 'seq'))
- input_grad: float32 [2048, 1536], P(('dp', 'seq'))
- grad_query: float32 [1536, 1536], P(('dp', 'seq'), 'mp')
- grad_key: float32 [1536, 256], P(('dp', 'seq', 'mp'))
- grad_value: float32 [1536, 256], P(('dp', 'seq', 'mp'))
- grad_bias_q: float32 [1536], P(('dp', 'seq', 'mp'))
- grad_bias_k: float32 [256], replicated
- grad_bias_v: float32 [256], P(('dp', 'seq', 'mp'))
- grad_out: float32 [1536, 1536], P('mp', ('dp', 'seq'))
- grad_gain_attn: float32 [1536], P(('dp', 'seq', 'mp'))
- grad_gain_ffn: float32 [1536], P(('dp', 'seq', 'mp'))
- grad_gate: float32 [1536, 8960], P(('dp', 'seq'), 'mp')
- grad_up: float32 [1536, 8960], P(('dp', 'seq'), 'mp')
- grad_down: float32 [8960, 1536], P('mp', ('dp', 'seq'))
The draws below stay inside these ranges and needn't reach their ends.
Inputs may be any that keep to these rules, and one draw needn't show every extreme that they name: `segments`: within each sequence of 512 tokens the ids never fall; a token attends only to tokens with its id; no document is longer than 256 tokens. `positions`: the index of each token within its document.
All inputs are finite; a program needn't handle non-finite values.
Results may differ from the reference program's by a relative error of at most 0.022.
The reference program's roundings to bfloat16 on the way count: a program that leaves them out, or rounds other values in their place, can miss the bound.
Values may be sent and summed in bfloat16 or wider, within the bound.
No kernel may reach another device: no remote copies, remote signals or barrier semaphores. Data moves between devices by JAX's collectives and lax.ppermute only.
A program may use at most 192 MiB of HBM per device.

```python
import math
import jax
import jax.numpy as jnp
from jax import lax

D = 1536
H = 12
KVH = 2
HD = 128
FF = 8960
LEN = 512
TOKENS = 2048


def document_cuts(key):
    seq_count = TOKENS // LEN
    first_cut = jax.random.randint(jax.random.fold_in(key, 11), (seq_count, 1), 1, LEN // 4 + 1)
    long_start = jax.random.randint(jax.random.fold_in(key, 12), (seq_count, 1), 1, LEN // 4 + 1)
    long_end = long_start + LEN // 2
    last_cut = jax.random.randint(jax.random.fold_in(key, 13), (seq_count, 1), 3 * LEN // 4, LEN)
    return jnp.concatenate([first_cut, long_start, long_end, last_cut], axis=1).astype(jnp.int32)


def draw_segments(key, part):
    cut_points = document_cuts(key)
    order = jnp.arange(LEN, dtype=jnp.int32)
    counted = jnp.sum((cut_points[:, None, :] <= order[None, :, None]).astype(jnp.int32), axis=-1)
    return counted.reshape(-1).astype(jnp.int32)


def draw_positions(key, part):
    cut_points = document_cuts(key)
    order = jnp.arange(LEN, dtype=jnp.int32)
    starts = jnp.max(jnp.where(cut_points[:, None, :] <= order[None, :, None], cut_points[:, None, :], 0), axis=-1)
    return (order[None, :] - starts).reshape(-1).astype(jnp.int32)


def bias_draw(key, heads_count, spread, limit):
    base = jnp.clip(spread * jax.random.normal(key, (heads_count, HD), jnp.float32), -limit, limit)
    return base.reshape(-1).astype(jnp.bfloat16)


def draw_bias_query(key, part):
    return bias_draw(jax.random.fold_in(key, 31), H, 0.3, 1.5)


def draw_bias_key(key, part):
    return bias_draw(jax.random.fold_in(key, 41), KVH, 1.0, 3.0)


def levels(own_key, extent, pieces, least, high):
    gain, own = 1.0, jax.random.fold_in(own_key, 6)
    for dim, shards_of in pieces:
        steps = jnp.exp(jax.random.uniform(jax.random.fold_in(own, dim), (shards_of,), jnp.float32, least / len(pieces), high / len(pieces)))
        gain = gain * jnp.repeat(steps, extent[dim] // shards_of).reshape([-1 if axis == dim else 1 for axis in range(len(extent))])
    return gain


def scatter_about(own_key, shape, deviation, bound, pieces=(), kind=jnp.bfloat16):
    gain = levels(own_key, shape, pieces, -0.22, 0.18) if pieces else 1.0
    entries = jax.random.normal(own_key, shape, jnp.float32) * deviation * gain
    return jnp.minimum(jnp.maximum(entries, -bound), bound).astype(kind)


def setup_inputs(seed: int = 0) -> dict:
    streams_of = jax.random.split(jax.random.key(seed), 17)
    return {
        "inputs": scatter_about(streams_of[0], (TOKENS, D), 1.0, 6.0, ((0, 8),)),
        "cotangent": scatter_about(streams_of[1], (TOKENS, D), 1.0, 6.0, ((0, 8),)),
        "segments": draw_segments(jax.random.fold_in(streams_of[16], 71), 0),
        "positions": draw_positions(jax.random.fold_in(streams_of[16], 71), 0),
        "w_query": scatter_about(streams_of[4], (D, H * HD), D ** -0.5, 0.15625, ((0, 8), (1, 4))),
        "w_key": scatter_about(streams_of[5], (D, KVH * HD), D ** -0.5, 0.15625, ((0, 32),)),
        "w_value": scatter_about(streams_of[6], (D, KVH * HD), D ** -0.5, 0.15625, ((0, 32),)),
        "bias_query": draw_bias_query(jax.random.fold_in(streams_of[16], 71), 0),
        "bias_key": draw_bias_key(jax.random.fold_in(streams_of[16], 71), 0),
        "bias_value": scatter_about(streams_of[9], (KVH * HD,), 0.5, 3.0, ((0, 32),)),
        "w_out": scatter_about(streams_of[10], (H * HD, D), (HD // 4) ** -0.5, 1.0, ((0, 4), (1, 8))),
        "gain_attn": jnp.clip(1.0 + 0.1 * jax.random.normal(streams_of[11], (D,), jnp.float32), 0.5, 1.5).astype(jnp.bfloat16),
        "gain_ffn": jnp.clip(1.0 + 0.1 * jax.random.normal(streams_of[12], (D,), jnp.float32), 0.5, 1.5).astype(jnp.bfloat16),
        "w_gate": scatter_about(streams_of[13], (D, FF), D ** -0.5, 0.15625, ((0, 8), (1, 4))),
        "w_up": scatter_about(streams_of[14], (D, FF), D ** -0.5, 0.15625, ((0, 8), (1, 4))),
        "w_down": scatter_about(streams_of[15], (FF, D), (FF // 64) ** -0.5, 0.5, ((0, 4), (1, 8))),
    }


EPSILON = 1e-06
ROPE_BASE = 1000000.0
NEG_BIG = -1e+30

def inverse_rms(values):
    return lax.rsqrt(lax.optimization_barrier(jnp.mean(values * values, axis=-1, keepdims=True)) + EPSILON)

def norm_backward(upstream, values, inv_scale, gain_vec):
    scaled = upstream * gain_vec
    return inv_scale * scaled - values * (inv_scale * inv_scale * inv_scale) * lax.optimization_barrier(jnp.mean(scaled * values, axis=-1, keepdims=True))

def rope_tables(positions):
    steps_half = jnp.arange(0, HD, 2).astype(jnp.float32)
    frequency = jnp.exp(steps_half * (-math.log(ROPE_BASE) / HD))
    angles = positions.astype(jnp.float32)[:, None] * frequency[None, :]
    angles = jnp.concatenate([angles, angles], axis=-1)
    return (jnp.cos(angles), jnp.sin(angles))

def rotate(values, cosine, sine_table):
    half_width = values.shape[-1] // 2
    turned = jnp.concatenate([-values[..., half_width:], values[..., :half_width]], axis=-1)
    return values * cosine + turned * sine_table

def head_forward(query_rows, key_rows, value_rows, mask_table, score_scale):
    scores = jnp.dot(query_rows, key_rows.T, preferred_element_type=jnp.float32) * score_scale
    scores = jnp.where(mask_table, scores, NEG_BIG)
    row_max = lax.optimization_barrier(jnp.max(scores, axis=-1, keepdims=True))
    row_total = lax.optimization_barrier(jnp.sum(jnp.where(mask_table, jnp.exp(scores - row_max), 0.0), axis=-1, keepdims=True))
    log_total = row_max + jnp.log(row_total)
    prob_cast = jnp.where(mask_table, jnp.exp(scores - log_total), 0.0).astype(jnp.bfloat16)
    attended = jnp.dot(prob_cast, value_rows, preferred_element_type=jnp.float32).astype(jnp.bfloat16)
    return (attended, log_total)

def head_backward(query_rows, key_rows, value_rows, mask_table, score_scale, log_total, attended, diff_attended):
    scores = jnp.dot(query_rows, key_rows.T, preferred_element_type=jnp.float32) * score_scale
    scores = jnp.where(mask_table, scores, NEG_BIG)
    prob_full = jnp.where(mask_table, jnp.exp(scores - log_total), 0.0)
    prob_cast = prob_full.astype(jnp.bfloat16)
    value_part = jnp.dot(prob_cast.T, diff_attended, preferred_element_type=jnp.float32)
    diff_probs = jnp.dot(diff_attended, value_rows.T, preferred_element_type=jnp.float32)
    row_delta = lax.optimization_barrier(jnp.sum(diff_attended.astype(jnp.float32) * attended.astype(jnp.float32), axis=-1, keepdims=True))
    diff_scores = (prob_full * (diff_probs - row_delta) * score_scale).astype(jnp.bfloat16)
    diff_query = jnp.dot(diff_scores, key_rows, preferred_element_type=jnp.float32)
    key_part = jnp.dot(diff_scores.T, query_rows, preferred_element_type=jnp.float32)
    return (diff_query, key_part, value_part)

def sequence_pass(inputs, cotangent, segments, positions, params):
    w_query, w_key, w_value, bias_query, bias_key, bias_value, w_out, gain_attn, gain_ffn, w_gate, w_up, w_down = params
    seq_rows = inputs.shape[0]
    group_size = H // KVH
    score_scale = HD ** (-0.5)
    in_float = inputs.astype(jnp.float32)
    inv_one = inverse_rms(in_float)
    normed_one = (in_float * inv_one * gain_attn.astype(jnp.float32)).astype(jnp.bfloat16)
    query_proj = jnp.dot(normed_one, w_query, preferred_element_type=jnp.float32) + bias_query.astype(jnp.float32)
    key_proj = jnp.dot(normed_one, w_key, preferred_element_type=jnp.float32) + bias_key.astype(jnp.float32)
    value_proj = jnp.dot(normed_one, w_value, preferred_element_type=jnp.float32) + bias_value.astype(jnp.float32)
    cosine, sine_table = rope_tables(positions)
    query_rot = rotate(query_proj.reshape(seq_rows, H, HD), cosine[:, None, :], sine_table[:, None, :]).astype(jnp.bfloat16)
    key_rot = rotate(key_proj.reshape(seq_rows, KVH, HD), cosine[:, None, :], sine_table[:, None, :]).astype(jnp.bfloat16)
    value_cast = value_proj.reshape(seq_rows, KVH, HD).astype(jnp.bfloat16)
    order = jnp.arange(seq_rows, dtype=jnp.int32)
    mask_table = (segments[:, None] == segments[None, :]) & (order[None, :] <= order[:, None])
    attended_list = []
    total_list = []
    for head_number in range(H):
        kv_number = head_number // group_size
        attended_head, total_head = head_forward(query_rot[:, head_number], key_rot[:, kv_number], value_cast[:, kv_number], mask_table, score_scale)
        attended_list.append(attended_head)
        total_list.append(total_head)
    attended_flat = jnp.concatenate(attended_list, axis=1)
    hidden_res = in_float + jnp.dot(attended_flat, w_out, preferred_element_type=jnp.float32)
    inv_two = inverse_rms(hidden_res)
    normed_two = (hidden_res * inv_two * gain_ffn.astype(jnp.float32)).astype(jnp.bfloat16)
    gate_proj = jnp.dot(normed_two, w_gate, preferred_element_type=jnp.float32)
    up_proj = jnp.dot(normed_two, w_up, preferred_element_type=jnp.float32)
    sigmoid_gate = jax.nn.sigmoid(gate_proj)
    silu_gate = gate_proj * sigmoid_gate
    hidden_act = (silu_gate * up_proj).astype(jnp.bfloat16)
    output = hidden_res + jnp.dot(hidden_act, w_down, preferred_element_type=jnp.float32)
    cot_float = cotangent.astype(jnp.float32)
    grad_down = jnp.dot(hidden_act.T, cotangent, preferred_element_type=jnp.float32)
    diff_hidden = jnp.dot(cotangent, w_down.T, preferred_element_type=jnp.float32)
    diff_gate = (diff_hidden * up_proj * sigmoid_gate * (1.0 + gate_proj * (1.0 - sigmoid_gate))).astype(jnp.bfloat16)
    diff_up = (diff_hidden * silu_gate).astype(jnp.bfloat16)
    grad_gate = jnp.dot(normed_two.T, diff_gate, preferred_element_type=jnp.float32)
    grad_up = jnp.dot(normed_two.T, diff_up, preferred_element_type=jnp.float32)
    diff_normed_two = jnp.dot(diff_gate, w_gate.T, preferred_element_type=jnp.float32) + jnp.dot(diff_up, w_up.T, preferred_element_type=jnp.float32)
    grad_gain_ffn = lax.optimization_barrier(jnp.sum(diff_normed_two * hidden_res * inv_two, axis=0))
    diff_res = cot_float + norm_backward(diff_normed_two, hidden_res, inv_two, gain_ffn.astype(jnp.float32))
    diff_res_cast = diff_res.astype(jnp.bfloat16)
    grad_out = jnp.dot(attended_flat.T, diff_res_cast, preferred_element_type=jnp.float32)
    diff_attended = jnp.dot(diff_res_cast, w_out.T, preferred_element_type=jnp.float32).astype(jnp.bfloat16)
    diff_attended = diff_attended.reshape(seq_rows, H, HD)
    query_list = []
    key_list = []
    value_list = []
    for head_number in range(H):
        kv_number = head_number // group_size
        diff_query, key_part, value_part = head_backward(query_rot[:, head_number], key_rot[:, kv_number], value_cast[:, kv_number], mask_table, score_scale, total_list[head_number], attended_list[head_number], diff_attended[:, head_number])
        query_list.append(diff_query)
        key_list.append(key_part)
        value_list.append(value_part)
    diff_query_all = jnp.stack(query_list, axis=1)
    key_all = jnp.stack(key_list, axis=1)
    value_all = jnp.stack(value_list, axis=1)
    query_pre = rotate(diff_query_all, cosine[:, None, :], -sine_table[:, None, :])
    key_pre = rotate(key_all, cosine[:, None, :], -sine_table[:, None, :])
    grad_bias_q = lax.optimization_barrier(jnp.sum(query_pre, axis=0)).reshape(H * HD)
    grad_bias_k = lax.optimization_barrier(jnp.sum(key_pre, axis=0)).reshape(KVH, group_size, HD).sum(axis=1).reshape(KVH * HD)
    grad_bias_v = lax.optimization_barrier(jnp.sum(value_all, axis=0)).reshape(KVH, group_size, HD).sum(axis=1).reshape(KVH * HD)
    query_cast = query_pre.reshape(seq_rows, H * HD).astype(jnp.bfloat16)
    key_cast = key_pre.reshape(seq_rows, H * HD).astype(jnp.bfloat16)
    value_cast_part = value_all.reshape(seq_rows, H * HD).astype(jnp.bfloat16)
    grad_query = jnp.dot(normed_one.T, query_cast, preferred_element_type=jnp.float32)
    grad_key = jnp.dot(normed_one.T, key_cast, preferred_element_type=jnp.float32).reshape(D, KVH, group_size, HD).sum(axis=2).reshape(D, KVH * HD)
    grad_value = jnp.dot(normed_one.T, value_cast_part, preferred_element_type=jnp.float32).reshape(D, KVH, group_size, HD).sum(axis=2).reshape(D, KVH * HD)
    key_repeat = jnp.repeat(w_key.reshape(D, KVH, HD), group_size, axis=1).reshape(D, H * HD)
    value_repeat = jnp.repeat(w_value.reshape(D, KVH, HD), group_size, axis=1).reshape(D, H * HD)
    diff_normed_one = jnp.dot(query_cast, w_query.T, preferred_element_type=jnp.float32) + jnp.dot(key_cast, key_repeat.T, preferred_element_type=jnp.float32) + jnp.dot(value_cast_part, value_repeat.T, preferred_element_type=jnp.float32)
    grad_gain_attn = lax.optimization_barrier(jnp.sum(diff_normed_one * in_float * inv_one, axis=0))
    input_grad = diff_res + norm_backward(diff_normed_one, in_float, inv_one, gain_attn.astype(jnp.float32))
    grads = (grad_query, grad_key, grad_value, grad_bias_q, grad_bias_k, grad_bias_v, grad_out, grad_gain_attn, grad_gain_ffn, grad_gate, grad_up, grad_down)
    return (output, input_grad, grads)

def reference(inputs, cotangent, segments, positions, w_query, w_key, w_value, bias_query, bias_key, bias_value, w_out, gain_attn, gain_ffn, w_gate, w_up, w_down):
    seq_count = inputs.shape[0] // LEN
    params = (w_query, w_key, w_value, bias_query, bias_key, bias_value, w_out, gain_attn, gain_ffn, w_gate, w_up, w_down)
    stacked = (inputs.reshape(seq_count, LEN, D), cotangent.reshape(seq_count, LEN, D), segments.reshape(seq_count, LEN), positions.reshape(seq_count, LEN))
    start_grads = (jnp.zeros((D, H * HD), jnp.float32), jnp.zeros((D, KVH * HD), jnp.float32), jnp.zeros((D, KVH * HD), jnp.float32), jnp.zeros((H * HD,), jnp.float32), jnp.zeros((KVH * HD,), jnp.float32), jnp.zeros((KVH * HD,), jnp.float32), jnp.zeros((H * HD, D), jnp.float32), jnp.zeros((D,), jnp.float32), jnp.zeros((D,), jnp.float32), jnp.zeros((D, FF), jnp.float32), jnp.zeros((D, FF), jnp.float32), jnp.zeros((FF, D), jnp.float32))

    def step_fn(carry, item):
        output, input_grad, grads = sequence_pass(item[0], item[1], item[2], item[3], params)
        summed = jax.tree.map(lambda first, second: first + second, carry, grads)
        return (summed, (output, input_grad))
    totals, (outputs, input_grads) = lax.scan(step_fn, start_grads, stacked)
    return (outputs.reshape(seq_count * LEN, D), input_grads.reshape(seq_count * LEN, D), totals[0], totals[1], totals[2], totals[3], totals[4], totals[5], totals[6], totals[7], totals[8], totals[9], totals[10], totals[11])
```

```python
import math

import jax
import jax.numpy as jnp
from jax import lax
from jax.experimental import pallas as pl
from jax.experimental.pallas import tpu as pltpu
from jax.sharding import PartitionSpec as P

D = 1536
H = 12
KVH = 2
HD = 128

EPSILON = 1e-06
ROPE_BASE = 1000000.0
NEG_BIG = -1e30
SMALL = 16
CHEAP = pl.CostEstimate(flops=0, bytes_accessed=0, transcendentals=0)
BF = jnp.bfloat16
F32 = jnp.float32


def dot(a, b):
    return jnp.dot(a, b, preferred_element_type=F32)


def dot_nt(a, b):
    return lax.dot_general(a, b, (((1,), (1,)), ((), ())), preferred_element_type=F32)


def dot_tn(a, b):
    return lax.dot_general(a, b, (((0,), (0,)), ((), ())), preferred_element_type=F32)


def inverse_rms(values):
    return lax.rsqrt(jnp.mean(values * values, axis=-1, keepdims=True) + EPSILON)


def norm_backward(upstream, values, inv_scale, gain_vec):
    scaled = upstream * gain_vec
    return inv_scale * scaled - values * (inv_scale * inv_scale * inv_scale) * jnp.mean(
        scaled * values, axis=-1, keepdims=True
    )


def rope_tables(positions):
    steps_half = jnp.arange(0, HD, 2).astype(F32)
    frequency = jnp.exp(steps_half * (-math.log(ROPE_BASE) / HD))
    angles = positions.astype(F32)[:, None] * frequency[None, :]
    angles = jnp.concatenate([angles, angles], axis=-1)
    return (jnp.cos(angles), jnp.sin(angles))


def head_backward(
    query_rows, key_rows, value_rows, mask_table, score_scale, log_total, attended, diff_attended
):
    scores = dot_nt(query_rows, key_rows) * score_scale + mask_table
    prob_full = jnp.exp(scores - log_total)
    prob_cast = prob_full.astype(BF)
    value_part = dot_tn(prob_cast, diff_attended)
    diff_probs = dot_nt(diff_attended, value_rows)
    row_delta = jnp.sum(
        diff_attended.astype(F32) * attended.astype(F32), axis=-1, keepdims=True
    )
    diff_scores = (prob_full * (diff_probs - row_delta) * score_scale).astype(BF)
    diff_query = dot(diff_scores, key_rows)
    key_part = dot_tn(diff_scores, query_rows)
    return (diff_query, key_part, value_part)


(
    ATTENDED,
    AWAY,
    BLOCKS,
    BOTH,
    BRANCH,
    BRANCH_C,
    BRANCH_HALF,
    BRANCH_Y,
    C,
    COT,
    COT_QUARTER,
    DIFF_NORMED,
    DIFF_RES,
    DN,
    DN1,
    DONE,
    DRES,
    FEED_AWAY,
    FEED_OWN,
    FFN,
    GRAD,
    GRADS_DONE,
    GRADS_FAR,
    GRADS_NEAR,
    G_SUM,
    G_X,
    G_Z,
    HALF,
    HEADS,
    HEADS_BACK,
    HIDDEN_AWAY,
    HIDDEN_OWN,
    HIDDEN_RES,
    INPUTS,
    INPUT_DIFF,
    INV_ONE,
    INV_QUARTER,
    INV_TWO,
    IN_FLOAT,
    IN_QUARTER,
    KV,
    KV_ACT_C,
    KV_ACT_X,
    KV_DONE_C,
    KV_DONE_HEADS,
    KV_DONE_Y,
    KV_GRADS,
    KV_GRAD_C,
    KV_GRAD_X,
    KV_PAIRS,
    KV_PRE,
    KV_ROT,
    KV_ROWS,
    KV_SEEN,
    KV_SLOTS,
    KV_SUM,
    KV_SUMS,
    LEFT,
    MASK,
    MASK_TABLE,
    N2,
    NORMED_ONE,
    NORMED_TWO,
    OUT,
    OUT_FULL,
    OWN,
    O_ALL,
    PAIR,
    PART,
    PAY,
    POSITIONS,
    PROJ,
    PROJECT,
    PROJECTED,
    QKV_CAST,
    QUERY,
    QUERY_PRE,
    QUERY_ROT,
    RESULTS,
    ROPE,
    SUMS,
    TOTAL,
    VECTOR,
    W_PREP,
    W_X,
    W_Z,
    X,
    X01,
    X10,
    XA,
    XB,
    XF,
    XN,
    Y,
    YA,
    YB,
    Z,
) = range(97)

AFTER = {
    (W_X, (0, 0)): [(O_ALL, X)],
    (O_ALL, (Z, 2)): [(QUERY, (Z, 2))],
    (QUERY, XB): [(O_ALL, (Z, 2))],
    (W_Z, (2, 0)): [(QUERY, (Z, 1))],
    (O_ALL, (Z, 1)): [(QUERY, (Z, 1))],
    PROJECT: [(W_Z, (2, 0)), (O_ALL, (Z, 1))],
    (COT, (Z, 2)): [(QUERY, XB)],
    (O_ALL, X): [(QUERY, XB)],
    KV_ACT_C: [(COT, (Z, 2))],
    (W_Z, (2, 1)): [KV_ACT_X],
    (COT, (Z, 1)): [KV_ACT_X],
    (W_X, (2, 0)): [BRANCH_Y],
    BRANCH_C: [(W_Z, (2, 1)), (COT, (Z, 1))],
    (W_Z, (2, 2)): [ATTENDED],
    (W_Z, (1, 0)): [ATTENDED],
    (W_X, (2, 1)): [(W_X, (2, 0))],
    (COT, YA): [ATTENDED],
    NORMED_TWO: [(W_Z, (2, 2)), (W_X, (0, 0)), (COT, YA)],
    (W_X, (2, 2)): [(W_X, (2, 1))],
    (COT, YB): [BRANCH_Y],
    (N2, (Z, 1)): [(W_Z, (1, 0)), (W_X, (2, 1)), (COT, YB)],
    (W_Z, (3, 0)): [(N2, (Z, 2))],
    (W_X, (1, 0)): [(N2, (Z, 2))],
    (N2, YB): [(W_Z, (3, 0))],
    (W_Z, (3, 1)): [(N2, (Z, 1))],
    (W_X, (3, 0)): [(W_X, (1, 0))],
    (COT, C): [(N2, (Z, 1))],
    (N2, C): [(W_Z, (3, 1)), (W_X, (1, 0))],
    (W_Z, (3, 2)): [(N2, YB)],
    (W_X, (3, 1)): [(W_X, (3, 0))],
    (W_X, (3, 2)): [(W_X, (3, 1))],
    INPUTS: [(QUERY, (Z, 2))],
    POSITIONS: [(QUERY, (Z, 2))],
    MASK: [(QUERY, (Z, 1))],
    W_PREP: [(KV, C)],
    GRADS_FAR: [(DN, OWN)],
    (DN, (Z, 1)): [GRADS_FAR],
    GRADS_NEAR: [(DN, YB)],
    (DN, (Z, 2)): [GRADS_NEAR],
    (G_X, 2): [(G_X, 3)],
    (DRES, Y): [(G_X, 3)],
    (FFN, AWAY): [(DN, (Z, 2))],
    (FFN, OWN): [(DN, (Z, 2))],
    (DRES, C): [(FFN, OWN), (FFN, AWAY)],
    (G_Z, (3, 0)): [(DN, (Z, 2))],
    HEADS_BACK: [(G_Z, (3, 0))],
    (G_X, 1): [(G_X, 2)],
    KV_GRAD_C: [(G_X, 2)],
    (G_Z, (3, 1)): [(DRES, C)],
    KV_GRAD_X: [(G_Z, (3, 1)), (FFN, C)],
    (FFN, C): [(DRES, C)],
    (G_Z, (3, 2)): [KV_GRAD_C],
    (PROJ, XF): [(G_X, 1)],
    (DN1, C): [(PROJ, GRAD)],
    (G_Z, (2, 0)): [(PROJ, GRAD)],
    (PROJ, (Z, 1)): [(G_Z, (3, 2)), (G_Z, (2, 0)), (FFN, YB), (DN1, Y)],
    (G_Z, (2, 1)): [(PROJ, XF)],
    (PROJ, (Z, 2)): [(G_Z, (2, 1)), (FFN, (Z, 1))],
    (VECTOR, C): [(PROJ, XF)],
    (OUT, X): [(PROJ, XF)],
    (G_Z, (2, 2)): [(PROJ, (Z, 1))],
    (G_Z, (1, 0)): [(G_Z, (3, 2))],
    KV_DONE_Y: [(G_Z, (2, 2)), (OUT, X), (VECTOR, Y), (G_Z, (1, 0))],
    (G_X, 0): [(OUT, X)],
    (OUT, GRAD): [KV_GRAD_C],
}


def after(x, *tokens):
    return lax.optimization_barrier((x, *tokens))[0] if tokens else x


def index(x, i, axis=0):
    return lax.dynamic_index_in_dim(x, i, axis, keepdims=False)


def split_columns(weights, n, pieces):
    rows, columns = weights[0].shape
    part, count = columns // n, len(weights)
    flat = [(j, cut) for j in range(n) for cut in pieces[j]]

    def kernel(*refs):
        ins, outs, held = refs[:count], refs[count:-1], refs[-1]
        d = lax.axis_index("dp")
        for i in range(count):
            for t in range(n):
                held[t] = ins[i][:, t * part : (t + 1) * part]
            for out, (j, (low, high)) in zip(outs, flat):
                out[i] = held[d ^ j, low:high]

    outs = pl.pallas_call(
        kernel,
        cost_estimate=CHEAP,
        out_shape=[
            jax.ShapeDtypeStruct((count, high - low, part), BF) for _, (low, high) in flat
        ],
        scratch_shapes=[pltpu.VMEM((n, rows, part), BF)],
        compiler_params=pltpu.CompilerParams(vmem_limit_bytes=48 << 20),
    )(*weights)
    return dict(zip(flat, outs))


def join_columns(blocks, n, rows):
    keys = list(blocks)
    count, _, part = blocks[keys[0]].shape

    def kernel(*refs):
        ins, outs, held = refs[: len(keys)], refs[len(keys) : -1], refs[-1]
        d = lax.axis_index("dp")
        for i in range(count):
            for ref, (j, (low, high)) in zip(ins, keys):
                held[d ^ j, low:high] = ref[i]
            for t in range(n):
                outs[i][:, t * part : (t + 1) * part] = held[t].astype(F32)

    return pl.pallas_call(
        kernel,
        cost_estimate=CHEAP,
        out_shape=[jax.ShapeDtypeStruct((rows, n * part), F32)] * count,
        scratch_shapes=[pltpu.VMEM((n, rows, part), BF)],
        compiler_params=pltpu.CompilerParams(vmem_limit_bytes=48 << 20),
    )(*blocks.values())


def key_value_slots(w_key, w_value, vectors):
    rows = w_key.shape[0]

    def kernel(key_ref, value_ref, *refs):
        ins, outs = refs[:-2], refs[-2:]
        head = lax.axis_index("mp") // (lax.axis_size("mp") // KVH)
        for i, ref in enumerate((key_ref, value_ref)):
            parts = [ref[:, k * HD : (k + 1) * HD] for k in range(KVH)]
            outs[0][i, :rows] = jnp.where(head == 0, parts[0], parts[1])
            outs[1][i, :rows] = jnp.where(head == 0, parts[1], parts[0])
            for out in outs:
                out[i, rows:] = jnp.zeros((SMALL, HD), BF)
                for j, vector in enumerate(ins):
                    out[i, rows + j : rows + j + 1, : vector.shape[1]] = vector[...]

    return pl.pallas_call(
        kernel, cost_estimate=CHEAP, out_shape=[jax.ShapeDtypeStruct((2, rows + SMALL, HD), BF)] * 2
    )(w_key, w_value, *[v[None] for v in vectors])


def join_rows(own, other, n_dp, n_seq, rows, lens):
    parts = [(a, o, 0) for a, o in own] + [(a, o, 1) for a, o in other]
    width = parts[0][0].shape[2]
    total = sum(len(o) for _, o, _ in parts)
    slots = n_dp * n_seq
    small = parts[0][0].shape[1] - rows

    def kernel(*refs):
        ins, out, vectors = refs[: len(parts)], refs[len(parts)], refs[len(parts) + 1 : -2]
        held, sem = refs[-2:]
        d = lax.axis_index("dp")
        s = lax.axis_index("seq")
        copies = []
        for ref, (_, offsets, side) in zip(ins, parts):
            for i, offset in enumerate(offsets):
                slot = (d ^ offset) * n_seq + (s ^ side)
                start = pl.multiple_of(slot * rows, rows)
                pairs = [(ref.at[i, pl.ds(0, rows)], out.at[pl.ds(start, rows)])]
                if lens:
                    pairs.append((ref.at[i, pl.ds(rows, small)], held.at[slot]))
                for pair in pairs:
                    copies.append(pltpu.make_async_copy(*pair, sem.at[len(copies)]))
        for copy in copies:
            copy.start()
        for copy in copies:
            copy.wait()
        for i, size in enumerate(lens):
            for t in range(slots):
                for k in range(small // SMALL):
                    at = (t * (small // SMALL) + k) * size
                    x = held[t, k * SMALL : (k + 1) * SMALL, :size].astype(F32)
                    vectors[i][:, at : at + size] = x[i : i + 1]

    return pl.pallas_call(
        kernel,
        cost_estimate=CHEAP,
        out_shape=[jax.ShapeDtypeStruct((slots * rows, width), BF)]
        + [jax.ShapeDtypeStruct((1, slots * (small // SMALL) * size), F32) for size in lens],
        in_specs=[pl.BlockSpec(memory_space=pl.ANY)] * len(parts),
        scratch_shapes=[
            pltpu.VMEM((slots, max(small, SMALL), width), BF),
            pltpu.SemaphoreType.DMA((2 * total,)),
        ],
    )(*[a for a, _, _ in parts])


def turn(x, cosine, sine_signed):
    return x * cosine + pltpu.roll(x, HD // 2, 1) * sine_signed


def project(x, vectors, w_q, w_kv, cosine, sine_signed):
    tokens = x.shape[0]
    wide = w_q.shape[1]

    def kernel(x_ref, bq, bk, bv, gain, _, w_ref, wkv_ref, cos_ref, sin_ref, *outs):
        normed, inv_ref, q_ref, kv_ref = outs
        m = lax.axis_index("mp")
        value = x_ref[...].astype(F32)
        inv = inverse_rms(value)
        inv_ref[...] = inv
        norm = (value * inv * gain[...]).astype(BF)
        normed[...] = norm
        proj = dot(norm, w_ref[...])
        cosine, sine = cos_ref[...], sin_ref[...]
        bias = bq[:, pl.ds(pl.multiple_of(m * wide, HD), wide)]
        for j in range(wide // HD):
            cut = slice(j * HD, (j + 1) * HD)
            q_ref[:, cut] = turn(proj[:, cut] + bias[:, cut], cosine, sine).astype(BF)
        head = pl.ds(pl.multiple_of((m // 2) * HD, HD), HD)
        last = dot(norm, wkv_ref[...]) + jnp.where(m % 2 == 0, bk[:, head], bv[:, head])
        kv_ref[...] = jnp.where(m % 2 == 0, turn(last, cosine, sine), last).astype(BF)

    return pl.pallas_call(
        kernel,
        cost_estimate=CHEAP,
        out_shape=[
            jax.ShapeDtypeStruct(x.shape, BF),
            jax.ShapeDtypeStruct((tokens, 1), F32),
            jax.ShapeDtypeStruct((tokens, wide), BF),
            jax.ShapeDtypeStruct((tokens, HD), BF),
        ],
    )(x, *vectors, w_q, w_kv, cosine, sine_signed)


def attend(query, seen, other, mask, out_t, quarter):
    tokens, wide = query.shape
    heads = wide // HD
    width = out_t.shape[0]

    def kernel(q_ref, seen_ref, other_ref, mask_ref, o_ref, att, log_ref, near, away, held):
        c = lax.axis_index("mp") % 2
        keys = jnp.where(c == 0, seen_ref[...], other_ref[...])
        vals = jnp.where(c == 0, other_ref[...], seen_ref[...])
        for j in range(heads):
            cut = slice(j * HD, (j + 1) * HD)
            scores = dot_nt(q_ref[:, cut], keys) * HD ** (-0.5) + mask_ref[...]
            top = jnp.max(scores, axis=-1, keepdims=True)
            total = jnp.sum(jnp.exp(scores - top), axis=-1, keepdims=True)
            log_total = top + jnp.log(total)
            log_ref[:, j : j + 1] = log_total
            att[:, cut] = dot(jnp.exp(scores - log_total).astype(BF), vals).astype(BF)
        held[...] = dot_nt(att[...], o_ref[...])
        for i in range(2):
            rows = pl.ds(pl.multiple_of((2 * i + c) * quarter, quarter), quarter)
            near[i] = held[rows]
            rows = pl.ds(pl.multiple_of((2 * i + 1 - c) * quarter, quarter), quarter)
            away[i] = held[rows].astype(BF)

    return pl.pallas_call(
        kernel,
        cost_estimate=CHEAP,
        out_shape=[
            jax.ShapeDtypeStruct((tokens, wide), BF),
            jax.ShapeDtypeStruct((tokens, heads), F32),
            jax.ShapeDtypeStruct((2, quarter, width), F32),
            jax.ShapeDtypeStruct((2, quarter, width), BF),
        ],
        scratch_shapes=[pltpu.VMEM((tokens, width), F32)],
    )(query, seen, other, mask, out_t)


def feed_rows(n2, cot, gate_ref, up_ref, down_ref, outs, waits):
    act, diff_gate_ref, diff_up_ref, dn = outs
    size = min(256, n2.shape[0])
    for i in range(n2.shape[0] // size):
        rows = slice(i * size, (i + 1) * size)
        if i == 0:
            waits[0]()
        gate_proj = dot(n2[rows], gate_ref[...])
        if i == 0:
            waits[1]()
        up_proj = dot(n2[rows], up_ref[...])
        if i == 0:
            waits[2]()
        diff_hidden = dot(cot[rows], down_ref[...])
        sigmoid_gate = 1.0 / (1.0 + jnp.exp(-gate_proj))
        silu_gate = gate_proj * sigmoid_gate
        act[rows] = (silu_gate * up_proj).astype(BF)
        diff_gate = (
            diff_hidden * up_proj * sigmoid_gate * (1.0 + gate_proj * (1.0 - sigmoid_gate))
        ).astype(BF)
        diff_up = (diff_hidden * silu_gate).astype(BF)
        diff_gate_ref[rows] = diff_gate
        diff_up_ref[rows] = diff_up
        dn[rows] = (dot_nt(diff_gate, gate_ref[...]) + dot_nt(diff_up, up_ref[...])).astype(dn.dtype)


def feed_shapes(n2, part, kind):
    shape = jax.ShapeDtypeStruct((n2.shape[0], part), BF)
    return [shape] * 3 + [jax.ShapeDtypeStruct(n2.shape, kind)]


def feed_limit(n2, part):
    part = -(-part // HD) * HD
    return min(60 << 20, (10 << 20) + 8 * n2.size + 12 * sum(n2.shape) * part)


def feed_first(n2, cot, blocks, rows, n_dp, n_seq):
    keys = list(blocks)
    part = blocks[keys[0]].shape[2]
    full = n_dp * n_seq * rows

    def kernel(n2_ref, cot_ref, *refs):
        ins, copies_out, outs = refs[: len(keys)], refs[len(keys) :][:3], refs[len(keys) + 3 :][:4]
        weights, sem = refs[-4:-1], refs[-1]
        d = lax.axis_index("dp")
        s = lax.axis_index("seq")
        back = [
            pltpu.make_async_copy(weights[w], copies_out[w], sem.at[w]) for w in range(3)
        ]

        def place(which):
            for ref, (side, j, (low, high)) in zip(ins, keys):
                size = high - low
                start = ((d ^ j) * n_seq + (s ^ side)) * rows + low
                weights[which][pl.ds(pl.multiple_of(start, size), size)] = ref[which]
            back[which].start()

        waits = [lambda w=w: place(w) for w in range(3)]
        feed_rows(n2_ref, cot_ref, *weights, outs, waits)
        for copy in back:
            copy.wait()

    whole = pl.BlockSpec(memory_space=pltpu.VMEM)
    return pl.pallas_call(
        kernel,
        cost_estimate=CHEAP,
        out_shape=[pltpu.HBM((full, part), BF)] * 3 + feed_shapes(n2, part, BF),
        out_specs=[pl.BlockSpec(memory_space=pltpu.HBM)] * 3 + [whole] * 4,
        scratch_shapes=[pltpu.VMEM((full, part), BF)] * 3
        + [pltpu.SemaphoreType.DMA((3,))],
        compiler_params=pltpu.CompilerParams(vmem_limit_bytes=feed_limit(n2, part)),
    )(n2, cot, *blocks.values())


def feed_second(n2, cot, gate, up, down):
    part = gate.shape[1]

    def kernel(n2_ref, cot_ref, gate_ref, up_ref, down_ref, *outs):
        feed_rows(n2_ref, cot_ref, gate_ref, up_ref, down_ref, outs, [lambda: None] * 3)

    return pl.pallas_call(
        kernel,
        cost_estimate=CHEAP,
        out_shape=feed_shapes(n2, part, F32),
        compiler_params=pltpu.CompilerParams(vmem_limit_bytes=feed_limit(n2, part)),
    )(n2, cot, gate, up, down)


def weight_grads(rows, which, diffs, n_dp, n_seq, far):
    count, half, n = len(diffs), n_dp // 2, 2 * len(rows)
    wide = rows[0][0].shape[1] // n_dp
    size, width = wide // n_seq, diffs[0][0].shape[1]
    operands = [a for pair in rows for a in pair] + [a for pair in diffs for a in pair]

    def kernel(*refs):
        ins, outs, held = refs[: len(operands)], refs[len(operands) : -1], refs[-1]
        d = lax.axis_index("dp")
        s = lax.axis_index("seq")
        upper = (d // half) ^ int(far)

        def columns(ref, t):
            if wide % HD == 0:
                start = upper * (half * wide) + t * wide
                return ref[:, pl.ds(pl.multiple_of(start, HD), wide)]
            low = ref[:, t * wide : (t + 1) * wide]
            high = ref[:, (half + t) * wide : (half + t + 1) * wide]
            return jnp.where(upper == 0, low, high)

        for i in range(count):
            for t in range(half):
                k = 2 * which[i]
                x = dot_tn(columns(ins[k], t), ins[n + 2 * i][...])
                x = x + dot_tn(columns(ins[k + 1], t), ins[n + 2 * i + 1][...])
                x = x.astype(BF)
                held[t, 0] = x[:size]
                held[t, 1] = x[size:]
            for j in range(half):
                outs[j][i] = held[(d % half) ^ j, s]
                outs[half + j][i] = held[(d % half) ^ j, 1 - s]

    total = sum(a.size for a in operands)
    need = (6 << 20) + (2 if total < 8 << 20 else 4) * total
    outs = pl.pallas_call(
        kernel,
        cost_estimate=CHEAP,
        out_shape=[jax.ShapeDtypeStruct((count, size, width), BF)] * n_dp,
        scratch_shapes=[pltpu.VMEM((half, n_seq, size, width), BF)],
        compiler_params=pltpu.CompilerParams(vmem_limit_bytes=min(60 << 20, need)),
    )(*operands)
    return outs[:half], outs[half:]


def token_grads(rows, diff, n_dp, n_seq, groups):
    wide = rows.shape[1] // n_dp
    size, width = wide // n_seq, diff.shape[1]

    def kernel(rows_ref, diff_ref, *refs):
        outs, held = refs[:-1], refs[-1]
        d = lax.axis_index("dp")
        s = lax.axis_index("seq")
        for t in range(n_dp):
            x = dot_tn(rows_ref[:, t * wide : (t + 1) * wide], diff_ref[...]).astype(BF)
            held[t, 0] = x[:size]
            held[t, 1] = x[size:]
        for side in range(2):
            for out, group in zip(outs[side * len(groups) :], groups):
                for i, offset in enumerate(group):
                    out[i] = held[d ^ offset, s ^ side]

    outs = pl.pallas_call(
        kernel,
        cost_estimate=CHEAP,
        out_shape=[jax.ShapeDtypeStruct((len(g), size, width), BF) for g in groups] * 2,
        scratch_shapes=[pltpu.VMEM((n_dp, n_seq, size, width), BF)],
    )(rows, diff)
    return outs[: len(groups)], outs[len(groups) :]


def solution(mesh):
    n_dp = mesh.shape["dp"]
    n_seq = mesh.shape["seq"]
    n_mp = mesh.shape["mp"]
    bits = [1 << i for i in reversed(range(n_dp.bit_length() - 1))]

    def on_device(
        inputs,
        cotangent,
        segments,
        positions,
        w_query,
        w_key,
        w_value,
        bias_query,
        bias_key,
        bias_value,
        w_out,
        gain_attn,
        gain_ffn,
        w_gate,
        w_up,
        w_down,
    ):
        d = lax.axis_index("dp")
        s = lax.axis_index("seq")
        m = lax.axis_index("mp")
        y, c = m // 2, m % 2
        tokens = inputs.shape[0]
        quarter = tokens // n_mp
        score_scale = HD ** (-0.5)
        wide = w_query.shape[1]
        heads_local = wide // HD
        rows_kv = w_key.shape[0]

        values, makers = {}, {}

        def get(name):
            if name not in values:
                values[name] = makers[name]()
            return values[name]

        def task(name):
            def add(maker):
                makers[name] = maker

            return add

        def tied(name, x):
            tokens = [jax.tree.leaves(get(o))[0] for o in AFTER.get(name, ()) if o in makers]
            return after(x, *tokens)

        links = {X: ("seq", [(0, 1), (1, 0)]), X01: ("seq", [(0, 1)]), X10: ("seq", [(1, 0)])}
        for k in range(1, n_dp):
            links[(Z, k)] = ("dp", [(j, j ^ k) for j in range(n_dp)])
        for k, name in ((1, C), (2, Y)):
            links[name] = ("mp", [(j, j ^ k) for j in range(n_mp)])

        def move(name, link, maker):
            makers[name] = lambda: lax.ppermute(tied(name, maker()), *links[link])

        def of(name):
            return lambda: get(name)

        def gather(name, maker, size, lens, split):
            makers[(name, PAY)] = lambda: maker()[None]
            pay, offsets = (name, PAY), [0]
            for k in bits[:-1]:
                recv = (name, (Z, k))
                move(recv, (Z, k), of(pay))
                makers[(recv, PAY)] = lambda a=pay, b=recv: jnp.concatenate([get(a), get(b)])
                pay, offsets = (recv, PAY), offsets + [o ^ k for o in offsets]
            k = bits[-1]
            recv = (name, (Z, k))
            move(recv, (Z, k), of(pay))
            there = [o ^ k for o in offsets]
            if split:
                move((name, XA), X, of(pay))
                move((name, XB), X, of(recv))
                own = lambda: [(get(pay), offsets), (get(recv), there)]
                other = lambda: [(get((name, XA)), offsets), (get((name, XB)), there)]
            else:
                makers[(name, BOTH)] = lambda: jnp.concatenate([get(pay), get(recv)])
                move((name, X), X, of((name, BOTH)))
                own = lambda: [(get((name, BOTH)), offsets + there)]
                other = lambda: [(get((name, X)), offsets + there)]
            makers[name] = lambda: join_rows(own(), other(), n_dp, n_seq, size, lens)

        w_rows = w_gate.shape[0]
        whole_cut = [(0, w_rows)]
        third = w_rows // 3
        third_cuts = [(i * third, (i + 1) * third) for i in range(3)]
        pieces = [whole_cut if k < n_dp // 2 else third_cuts for k in range(n_dp)]
        tails = [(k, cut, (k, i)) for k in range(n_dp) for i, cut in enumerate(pieces[k])]
        makers[W_PREP] = lambda: split_columns(
            [tied(W_PREP, w_gate), w_up, w_down.T], n_dp, pieces
        )
        for k, cut, tail in tails:
            if k:
                move((W_Z, tail), (Z, k), lambda k=k, cut=cut: get(W_PREP)[k, cut])
            else:
                makers[(W_Z, tail)] = lambda cut=cut: get(W_PREP)[0, cut]
            move((W_X, tail), X, of((W_Z, tail)))

        def rows_gather(name, maker):
            makers[(name, PAY)] = maker
            pay = (name, PAY)
            for k in bits[:-1]:
                recv = (name, (Z, k))
                move(recv, (Z, k), of(pay))
                makers[(recv, PAY)] = lambda a=pay, b=recv: jnp.concatenate([get(a), get(b)])
                pay = (recv, PAY)
            recv = (name, (Z, bits[-1]))
            move(recv, (Z, bits[-1]), of(pay))
            move((name, YA), Y, of(pay))
            move((name, YB), Y, of(recv))
            makers[(name, OWN)] = lambda: jnp.concatenate(
                [get(pay), get(recv), get((name, YA)), get((name, YB))]
            )
            move((name, C), C, of((name, OWN)))

        def rows_sum(name):
            move((name, C), C, of((name, AWAY)))
            last = (name, (Z, bits[-1]))

            def part(i):
                size = get((name, OWN)).shape[0] // 4
                cut = slice(i * size, (i + 1) * size)
                return get((name, OWN))[cut] + get((name, C))[cut].astype(F32)

            for i in range(4):
                makers[(name, PART, i)] = lambda i=i: part(i)
            move((name, YB), Y, lambda: get((name, PART, 3)).astype(BF))
            move((name, YA), Y, lambda: get((name, PART, 2)).astype(BF))
            move(
                last,
                (Z, bits[-1]),
                lambda: (get((name, PART, 1)) + get((name, YB)).astype(F32)).astype(BF),
            )
            makers[(name, LEFT, 0)] = (
                lambda: get((name, PART, 0)) + get((name, YA)).astype(F32) + get(last).astype(F32)
            )
            left = (name, LEFT, 0)
            for i, k in enumerate(reversed(bits[:-1])):
                recv = (name, (Z, k))

                def far(left=left):
                    return get(left)[get(left).shape[0] // 2 :].astype(BF)

                def near(left=left, recv=recv):
                    return get(left)[: get(left).shape[0] // 2] + get(recv).astype(F32)

                move(recv, (Z, k), far)
                left = (name, LEFT, i + 1)
                makers[left] = near
            makers[name] = of(left)

        def weight_grad_ways(name, far):
            own, away = get(HIDDEN_OWN), get(HIDDEN_AWAY)
            n2 = [tied(name, get((N2, OWN))), get((N2, C))]
            cot = [get((COT, OWN)), get((COT, C))]
            return weight_grads(
                [n2, cot],
                [0, 0, 1],
                [[own[1], away[1]], [own[2], away[2]], [own[0], away[0]]],
                n_dp,
                n_seq,
                far,
            )

        makers[GRADS_FAR] = lambda: weight_grad_ways(GRADS_FAR, True)
        makers[GRADS_NEAR] = lambda: weight_grad_ways(GRADS_NEAR, False)

        def grad_piece(k, side):
            return get(GRADS_NEAR if k < n_dp // 2 else GRADS_FAR)[side][k % (n_dp // 2)]

        for k in range(n_dp):
            move((G_X, k), X, lambda k=k: grad_piece(k, 1))
        for k, cut, tail in tails:

            def summed(k=k, cut=cut, tail=tail):
                low, high = cut
                own = tied((G_SUM, tail), grad_piece(k, 0)[:, low:high]).astype(F32)
                return (own + get((G_X, k))[:, low:high].astype(F32)).astype(BF)

            makers[(G_SUM, tail)] = summed
            if k:
                move((G_Z, tail), (Z, k), of((G_SUM, tail)))
            else:
                makers[(G_Z, tail)] = of((G_SUM, tail))
        makers[GRADS_DONE] = lambda: join_columns(
            {(k, cut): get((G_Z, tail)) for k, cut, tail in tails}, n_dp, w_rows
        )

        def gather_grad(name, rows, diff, split):
            near = [0]
            for k in bits[:-1]:
                near = near + [o ^ k for o in near]
            far = [o ^ bits[-1] for o in near]
            n_near = len(near)
            groups = [near, far] if split else [near + far]
            makers[(name, GRAD)] = lambda: token_grads(rows(), diff(), n_dp, n_seq, groups)
            if split:
                move((name, XF), X, lambda: get((name, GRAD))[1][1])
                move((name, XN), X, lambda: get((name, GRAD))[1][0])
                own = lambda i: get((name, GRAD))[0][i]
            else:
                move((name, X), X, lambda: get((name, GRAD))[1][0])
                makers[(name, XN)] = lambda: get((name, X))[:n_near]
                makers[(name, XF)] = lambda: get((name, X))[n_near:]
                own = lambda i: get((name, GRAD))[0][0][i * n_near : (i + 1) * n_near]

            def both(i, recv):
                return own(i).astype(F32) + get(recv).astype(F32)

            last = (name, (Z, bits[-1]))
            move(last, (Z, bits[-1]), lambda: both(1, (name, XF)).astype(BF))
            makers[(name, LEFT, 0)] = lambda: both(0, (name, XN)) + get(last).astype(F32)
            left = (name, LEFT, 0)
            for i, k in enumerate(reversed(bits[:-1])):
                recv = (name, (Z, k))

                def far_half(left=left):
                    return get(left)[get(left).shape[0] // 2 :].astype(BF)

                def near_half(left=left, recv=recv):
                    return get(left)[: get(left).shape[0] // 2] + get(recv).astype(F32)

                move(recv, (Z, k), far_half)
                left = (name, LEFT, i + 1)
                makers[left] = near_half
            makers[(name, DONE)] = lambda: get(left)[0]

        def mp_gather(name, maker):
            move((name, Y), Y, maker)

            def pair():
                a, b = maker(), get((name, Y))
                return jnp.where(y == 0, jnp.stack([a, b]), jnp.stack([b, a]))

            makers[(name, PAIR)] = pair
            move((name, C), C, of((name, PAIR)))

            def whole():
                a, b = get((name, PAIR)), get((name, C))
                both = jnp.where(c == 0, jnp.stack([a, b], axis=1), jnp.stack([b, a], axis=1))
                return both.reshape(-1, both.shape[-1])

            makers[name] = whole

        def mp_sum(name, maker):
            def blocks():
                x = maker()
                return x.reshape(2, 2, -1, x.shape[-1])

            makers[(name, BLOCKS)] = blocks
            move((name, C), C, lambda: index(get((name, BLOCKS)), 1 - c, 1).astype(BF))
            makers[(name, HALF)] = lambda: index(get((name, BLOCKS)), c, 1) + get(
                (name, C)
            ).astype(F32)
            move((name, Y), Y, lambda: index(get((name, HALF)), 1 - y).astype(BF))
            makers[name] = lambda: index(get((name, HALF)), y) + get((name, Y)).astype(F32)

        gather(QUERY, lambda: w_query, w_query.shape[0], [], True)
        gather(O_ALL, lambda: tied(O_ALL, w_out).T, w_query.shape[0], [], False)
        makers[OUT_FULL] = lambda: get(O_ALL)[0]

        vectors = (bias_query, bias_key, bias_value, gain_attn, gain_ffn)

        makers[KV_SLOTS] = lambda: key_value_slots(w_key, w_value, vectors)
        move((KV, Y), Y, lambda: get(KV_SLOTS)[1])

        @task(KV_PAIRS)
        def kv_pairs():
            return jnp.stack([get(KV_SLOTS)[0], get((KV, Y))])

        move((KV, C), C, lambda: index(get(KV_PAIRS), 1 - c, 1))

        @task(KV_ROWS)
        def kv_rows():
            own, got = index(get(KV_PAIRS), c, 1), get((KV, C))
            by_core = jnp.where(
                c == 0, jnp.stack([own, got], axis=1), jnp.stack([got, own], axis=1)
            )
            whole = jnp.where(y == 0, by_core, by_core[::-1])
            parts = [whole[:, :, :rows_kv], whole[:, :, rows_kv:]]
            return jnp.concatenate([x.reshape(-1, HD) for x in parts])

        gather(
            KV, of(KV_ROWS), n_mp * rows_kv, [v.shape[0] for v in vectors], False
        )

        @task(IN_FLOAT)
        def in_float():
            return tied(INPUTS, inputs).astype(F32)

        @task(ROPE)
        def rope():
            cosine, sine_table = rope_tables(tied(POSITIONS, positions))
            first = jnp.arange(HD) < HD // 2
            return cosine, jnp.where(first, -sine_table, sine_table)

        @task(PROJECTED)
        def projected():
            weights, *small = get(KV)
            x = tied(PROJECT, inputs)
            return project(x, small, get(QUERY)[0], weights, *get(ROPE))

        makers[NORMED_ONE] = lambda: get(PROJECTED)[0]
        makers[INV_ONE] = lambda: get(PROJECTED)[1]
        makers[QUERY_ROT] = lambda: get(PROJECTED)[2]
        makers[KV_ROT] = lambda: tied(KV_ROT, get(PROJECTED)[3])

        move(KV_ACT_X, X01, of(KV_ROT))

        @task(KV_SEEN)
        def kv_seen():
            return jnp.concatenate([get(KV_ACT_X), get(KV_ROT)], axis=0)

        move(KV_ACT_C, C, of(KV_SEEN))

        @task(MASK_TABLE)
        def mask_table():
            where = tied(MASK, segments)
            seg_before = where[:tokens]
            seg_own = lax.dynamic_slice_in_dim(where, s * tokens, tokens, 0)
            order = jnp.arange(tokens, dtype=jnp.int32)
            before = (seg_own[:, None] == seg_before[None, :]) & (s > 0)
            own = (seg_own[:, None] == seg_own[None, :]) & (order[None, :] <= order[:, None])
            return jnp.where(jnp.concatenate([before, own], axis=1), 0.0, NEG_BIG)

        @task(HEADS)
        def heads():
            return attend(
                get(QUERY_ROT),
                get(KV_SEEN),
                tied(HEADS, get(KV_ACT_C)),
                get(MASK_TABLE),
                get(OUT_FULL),
                quarter,
            )

        makers[ATTENDED] = lambda: get(HEADS)[0]

        move(BRANCH_C, C, lambda: get(HEADS)[3])
        makers[BRANCH_HALF] = lambda: get(HEADS)[2] + get(BRANCH_C).astype(F32)
        move(BRANCH_Y, Y, lambda: index(get(BRANCH_HALF), 1 - y).astype(BF))
        makers[BRANCH] = lambda: index(get(BRANCH_HALF), y) + get(BRANCH_Y).astype(F32)

        @task(IN_QUARTER)
        def in_quarter():
            return lax.dynamic_slice_in_dim(get(IN_FLOAT), m * quarter, quarter, 0)

        @task(HIDDEN_RES)
        def hidden_res():
            return get(IN_QUARTER) + get(BRANCH)

        @task(INV_TWO)
        def inv_two():
            return inverse_rms(get(HIDDEN_RES))

        @task(NORMED_TWO)
        def normed_two():
            return tied(
                NORMED_TWO, (get(HIDDEN_RES) * get(INV_TWO) * get(KV)[5]).astype(BF)
            )

        @task(COT_QUARTER)
        def cot_quarter():
            return lax.dynamic_slice_in_dim(cotangent, m * quarter, quarter, 0)

        rows_gather(N2, of(NORMED_TWO))
        rows_gather(COT, of(COT_QUARTER))

        @task(FEED_AWAY)
        def feed_away():
            blocks = {(0, k, cut): get((W_Z, tail)) for k, cut, tail in tails}
            blocks.update({(1, k, cut): get((W_X, tail)) for k, cut, tail in tails})
            return feed_first(
                tied(FEED_AWAY, get((N2, C))), get((COT, C)), blocks, w_rows, n_dp, n_seq
            )

        @task(FEED_OWN)
        def feed_own():
            weights = get(FEED_AWAY)[:3]
            return feed_second(tied(FEED_OWN, get((N2, OWN))), get((COT, OWN)), *weights)

        makers[HIDDEN_AWAY] = lambda: get(FEED_AWAY)[3:6]
        makers[HIDDEN_OWN] = lambda: get(FEED_OWN)[:3]
        makers[(DN, AWAY)] = lambda: get(FEED_AWAY)[6]
        makers[(DN, OWN)] = lambda: get(FEED_OWN)[3]
        makers[(FFN, OWN)] = lambda: dot_nt(
            tied((FFN, OWN), get(HIDDEN_OWN)[0]), get(FEED_AWAY)[2]
        )
        makers[(FFN, AWAY)] = lambda: dot_nt(
            tied((FFN, AWAY), get(HIDDEN_AWAY)[0]), get(FEED_AWAY)[2]
        ).astype(BF)
        rows_sum(DN)

        rows_sum(FFN)

        @task(DIFF_RES)
        def diff_res():
            return get(COT_QUARTER).astype(F32) + norm_backward(
                get(DN), get(HIDDEN_RES), get(INV_TWO), get(KV)[5]
            )

        mp_gather(DRES, lambda: get(DIFF_RES).astype(BF))

        @task(HEADS_BACK)
        def heads_back():
            seen, other = get(KV_SEEN), get(KV_ACT_C)
            keys, vals = jnp.where(c == 0, seen, other), jnp.where(c == 0, other, seen)
            queries, logs = get(QUERY_ROT), get(HEADS)[1]
            diff_attended = tied(HEADS_BACK, dot(get(DRES), get(OUT_FULL)).astype(BF))
            return [
                head_backward(
                    queries[:, j * HD : (j + 1) * HD],
                    keys,
                    vals,
                    get(MASK_TABLE),
                    score_scale,
                    logs[:, j : j + 1],
                    get(ATTENDED)[:, j * HD : (j + 1) * HD],
                    diff_attended[:, j * HD : (j + 1) * HD],
                )
                for j in range(heads_local)
            ]

        @task(KV_SUMS)
        def kv_sums():
            return [sum(head[i] for head in get(HEADS_BACK)) for i in (1, 2)]

        move(KV_GRAD_C, C, lambda: jnp.where(c == 0, *reversed(get(KV_SUMS))))

        @task(KV_SUM)
        def kv_sum():
            return jnp.where(c == 0, *get(KV_SUMS)) + get(KV_GRAD_C)

        move(KV_GRAD_X, X10, lambda: get(KV_SUM)[:tokens])

        def turn_back(x):
            cosine, sine_signed = get(ROPE)
            return x * cosine - jnp.roll(x, HD // 2, axis=1) * sine_signed

        @task(KV_PRE)
        def kv_pre():
            mine = get(KV_SUM)[tokens:] + get(KV_GRAD_X)
            return jnp.where(c == 0, turn_back(mine), mine)

        @task(QUERY_PRE)
        def query_pre():
            return jnp.concatenate([turn_back(head[0]) for head in get(HEADS_BACK)], axis=1)

        @task(QKV_CAST)
        def qkv_cast():
            return jnp.concatenate([get(QUERY_PRE), get(KV_PRE)], axis=1).astype(BF)

        gather_grad(PROJ, of(NORMED_ONE), of(QKV_CAST), True)
        gather_grad(OUT, lambda: tied((OUT, GRAD), get(DRES)), of(ATTENDED), False)

        @task(DIFF_NORMED)
        def diff_normed():
            cast = get(QKV_CAST)
            return dot_nt(cast[:, :wide], get(QUERY)[0]) + dot_nt(cast[:, wide:], get(KV)[0])

        mp_sum(DN1, of(DIFF_NORMED))

        @task((KV, DONE))
        def kv_done():
            return get((PROJ, DONE))[:, wide:].reshape(2, 2, rows_kv, HD).astype(BF)

        move(KV_DONE_Y, Y, lambda: index(get((KV, DONE)), 1 - y))

        @task(KV_DONE_HEADS)
        def kv_done_heads():
            mine, got = index(get((KV, DONE)), y), get(KV_DONE_Y)
            return jnp.where(y == 0, jnp.stack([mine, got]), jnp.stack([got, mine]))

        move(KV_DONE_C, C, lambda: index(get(KV_DONE_HEADS), 1 - c, 1))

        @task(KV_GRADS)
        def kv_grads():
            mine, got = index(get(KV_DONE_HEADS), c, 1), get(KV_DONE_C)
            return [
                jnp.where(c == 0, a, b)
                .transpose(1, 0, 2)
                .reshape(rows_kv, KVH * HD)
                .astype(F32)
                for a, b in ((mine, got), (got, mine))
            ]

        @task(INV_QUARTER)
        def inv_quarter():
            return lax.dynamic_slice_in_dim(get(INV_ONE), m * quarter, quarter, 0)

        @task(INPUT_DIFF)
        def input_diff():
            return get(DIFF_RES) + norm_backward(
                get(DN1), get(IN_QUARTER), get(INV_QUARTER), get(KV)[4]
            )

        mp_gather(
            RESULTS,
            lambda: jnp.concatenate(
                [get(HIDDEN_RES) + get(FFN), get(INPUT_DIFF)], axis=1
            ).astype(BF),
        )

        @task(VECTOR)
        def vector():
            grad_gain_ffn = jnp.sum(get(DN) * get(HIDDEN_RES) * get(INV_TWO), axis=0)
            grad_gain_attn = jnp.sum(get(DN1) * get(IN_QUARTER) * get(INV_QUARTER), axis=0)
            grad_bq = jnp.sum(get(QUERY_PRE), axis=0)
            grad_bkv = jnp.sum(get(KV_PRE), axis=0)
            zeros_kv = jnp.zeros((2, KVH, HD), F32)
            return jnp.concatenate(
                [
                    lax.dynamic_update_slice_in_dim(
                        jnp.zeros((H * HD,), F32), grad_bq, m * wide, 0
                    ),
                    grad_gain_attn,
                    grad_gain_ffn,
                    lax.dynamic_update_slice(zeros_kv, grad_bkv[None, None], (c, y, 0)).reshape(-1),
                ]
            ).reshape(-1, HD)

        total = VECTOR
        for link in [C, Y, X] + [(Z, k) for k in bits]:
            move((VECTOR, link), link, of(total))
            makers[(TOTAL, link)] = lambda a=total, b=(VECTOR, link): get(a) + get(b)
            total = (TOTAL, link)

        makers[SUMS] = lambda: get(total).reshape(-1)
        device = (d * n_seq + s) * n_mp + m

        def own(start, length):
            width = length // (n_dp * n_seq * n_mp)
            return lax.dynamic_slice_in_dim(
                get(SUMS)[start : start + length], device * width, width, 0
            )

        return (
            get(RESULTS)[:, :D].astype(F32),
            get(RESULTS)[:, D:].astype(F32),
            get((PROJ, DONE))[:, :wide],
            get(KV_GRADS)[0],
            get(KV_GRADS)[1],
            own(0, H * HD),
            get(SUMS)[3 * D : 3 * D + KVH * HD],
            own(3 * D + KVH * HD, KVH * HD),
            get((OUT, DONE)).T,
            own(D, D),
            own(2 * D, D),
            get(GRADS_DONE)[0],
            get(GRADS_DONE)[1],
            get(GRADS_DONE)[2].T,
        )

    in_specs = (
        P(("dp", "seq"), None),
        P(("dp", "seq"), None),
        P("dp"),
        P(("dp", "seq")),
        P(("dp", "seq"), "mp"),
        P(("dp", "seq", "mp"), None),
        P(("dp", "seq", "mp"), None),
        P(("dp", "seq", "mp")),
        P(("dp", "seq", "mp")),
        P(("dp", "seq", "mp")),
        P("mp", ("dp", "seq")),
        P(("dp", "seq", "mp")),
        P(("dp", "seq", "mp")),
        P(("dp", "seq"), "mp"),
        P(("dp", "seq"), "mp"),
        P("mp", ("dp", "seq")),
    )
    out_specs = (
        P(("dp", "seq"), None),
        P(("dp", "seq"), None),
        P(("dp", "seq"), "mp"),
        P(("dp", "seq", "mp"), None),
        P(("dp", "seq", "mp"), None),
        P(("dp", "seq", "mp")),
        P(),
        P(("dp", "seq", "mp")),
        P("mp", ("dp", "seq")),
        P(("dp", "seq", "mp")),
        P(("dp", "seq", "mp")),
        P(("dp", "seq"), "mp"),
        P(("dp", "seq"), "mp"),
        P("mp", ("dp", "seq")),
    )
    return jax.shard_map(
        on_device, mesh=mesh, in_specs=in_specs, out_specs=out_specs, check_vma=False
    )
```

```python
import math

import jax
import jax.numpy as jnp
from jax import lax
from jax.experimental import pallas as pl
from jax.experimental.pallas import tpu as pltpu
from jax.sharding import PartitionSpec as P

D = 1536
H = 12
KVH = 2
HD = 128

EPSILON = 1e-06
ROPE_BASE = 1000000.0
NEG_BIG = -1e30
SMALL = 16
CHEAP = pl.CostEstimate(flops=0, bytes_accessed=0, transcendentals=0)
BF = jnp.bfloat16
F32 = jnp.float32


def dot(a, b):
    return jnp.dot(a, b, preferred_element_type=F32)


def dot_nt(a, b):
    return lax.dot_general(a, b, (((1,), (1,)), ((), ())), preferred_element_type=F32)


def dot_tn(a, b):
    return lax.dot_general(a, b, (((0,), (0,)), ((), ())), preferred_element_type=F32)


def inverse_rms(values):
    return lax.rsqrt(jnp.mean(values * values, axis=-1, keepdims=True) + EPSILON)


def norm_backward(upstream, values, inv_scale, gain_vec):
    scaled = upstream * gain_vec
    return inv_scale * scaled - values * (inv_scale * inv_scale * inv_scale) * jnp.mean(
        scaled * values, axis=-1, keepdims=True
    )


def rope_tables(positions):
    steps_half = jnp.arange(0, HD, 2).astype(F32)
    frequency = jnp.exp(steps_half * (-math.log(ROPE_BASE) / HD))
    angles = positions.astype(F32)[:, None] * frequency[None, :]
    angles = jnp.concatenate([angles, angles], axis=-1)
    return (jnp.cos(angles), jnp.sin(angles))


def head_backward(
    query_rows, key_rows, value_rows, mask_table, score_scale, log_total, attended, diff_attended
):
    scores = dot_nt(query_rows, key_rows) * score_scale + mask_table
    prob_full = jnp.exp(scores - log_total)
    prob_cast = prob_full.astype(BF)
    value_part = dot_tn(prob_cast, diff_attended)
    diff_probs = dot_nt(diff_attended, value_rows)
    row_delta = jnp.sum(
        diff_attended.astype(F32) * attended.astype(F32), axis=-1, keepdims=True
    )
    diff_scores = (prob_full * (diff_probs - row_delta) * score_scale).astype(BF)
    diff_query = dot(diff_scores, key_rows)
    key_part = dot_tn(diff_scores, query_rows)
    return (diff_query, key_part, value_part)


(
    ATTENDED,
    AWAY,
    BLOCKS,
    BOTH,
    BRANCH,
    BRANCH_C,
    BRANCH_HALF,
    BRANCH_Y,
    C,
    COT,
    COT_QUARTER,
    DIFF_NORMED,
    DIFF_RES,
    DN,
    DN1,
    DONE,
    DRES,
    FEED_AWAY,
    FEED_OWN,
    FFN,
    GRAD,
    GRADS_DONE,
    GRADS_FAR,
    GRADS_NEAR,
    G_SUM,
    G_X,
    G_Z,
    HALF,
    HEADS,
    HEADS_BACK,
    HIDDEN_AWAY,
    HIDDEN_OWN,
    HIDDEN_RES,
    INPUTS,
    INPUT_DIFF,
    INV_ONE,
    INV_QUARTER,
    INV_TWO,
    IN_FLOAT,
    IN_QUARTER,
    KV,
    KV_ACT_C,
    KV_ACT_X,
    KV_DONE_C,
    KV_DONE_HEADS,
    KV_DONE_Y,
    KV_GRADS,
    KV_GRAD_C,
    KV_GRAD_X,
    KV_PAIRS,
    KV_PRE,
    KV_ROT,
    KV_ROWS,
    KV_SEEN,
    KV_SLOTS,
    KV_SUM,
    KV_SUMS,
    LEFT,
    MASK,
    MASK_TABLE,
    N2,
    NORMED_ONE,
    NORMED_TWO,
    OUT,
    OUT_FULL,
    OWN,
    O_ALL,
    PAIR,
    PART,
    PAY,
    POSITIONS,
    PROJ,
    PROJECT,
    PROJECTED,
    QKV_CAST,
    QUERY,
    QUERY_PRE,
    QUERY_ROT,
    RESULTS,
    ROPE,
    SUMS,
    TOTAL,
    VECTOR,
    W_PREP,
    W_X,
    W_Z,
    X,
    X01,
    X10,
    XA,
    XB,
    XF,
    XN,
    Y,
    YA,
    YB,
    Z,
) = range(97)

AFTER = {
    (W_X, (0, 0)): [(O_ALL, X)],
    (O_ALL, (Z, 2)): [(QUERY, (Z, 2))],
    (QUERY, XB): [(O_ALL, (Z, 2))],
    (W_Z, (2, 0)): [(QUERY, (Z, 1))],
    (O_ALL, (Z, 1)): [(QUERY, (Z, 1))],
    PROJECT: [(W_Z, (2, 0)), (O_ALL, (Z, 1))],
    (COT, (Z, 2)): [(QUERY, XB)],
    (O_ALL, X): [(QUERY, XB)],
    KV_ACT_C: [(COT, (Z, 2))],
    (W_Z, (2, 1)): [KV_ACT_X],
    (COT, (Z, 1)): [KV_ACT_X],
    (W_X, (2, 0)): [BRANCH_Y],
    BRANCH_C: [(W_Z, (2, 1)), (COT, (Z, 1))],
    (W_Z, (2, 2)): [ATTENDED],
    (W_Z, (1, 0)): [ATTENDED],
    (W_X, (2, 1)): [(W_X, (2, 0))],
    (COT, YA): [ATTENDED],
    NORMED_TWO: [(W_Z, (2, 2)), (W_X, (0, 0)), (COT, YA)],
    (W_X, (2, 2)): [(W_X, (2, 1))],
    (COT, YB): [BRANCH_Y],
    (N2, (Z, 1)): [(W_Z, (1, 0)), (W_X, (2, 1)), (COT, YB)],
    (W_Z, (3, 0)): [(N2, (Z, 2))],
    (W_X, (1, 0)): [(N2, (Z, 2))],
    (N2, YB): [(W_Z, (3, 0))],
    (W_Z, (3, 1)): [(N2, (Z, 1))],
    (W_X, (3, 0)): [(W_X, (1, 0))],
    (COT, C): [(N2, (Z, 1))],
    (N2, C): [(W_Z, (3, 1)), (W_X, (1, 0))],
    (W_Z, (3, 2)): [(N2, YB)],
    (W_X, (3, 1)): [(W_X, (3, 0))],
    (W_X, (3, 2)): [(W_X, (3, 1))],
    INPUTS: [(QUERY, (Z, 2))],
    POSITIONS: [(QUERY, (Z, 2))],
    MASK: [(QUERY, (Z, 1))],
    W_PREP: [(KV, C)],
    GRADS_FAR: [(DN, OWN)],
    (DN, (Z, 1)): [GRADS_FAR],
    GRADS_NEAR: [(DN, YB)],
    (DN, (Z, 2)): [GRADS_NEAR],
    (G_X, 2): [(G_X, 3)],
    (DRES, Y): [(G_X, 3)],
    (FFN, AWAY): [(DN, (Z, 2))],
    (FFN, OWN): [(DN, (Z, 2))],
    (DRES, C): [(FFN, OWN), (FFN, AWAY)],
    (G_Z, 3): [(DN, (Z, 2))],
    (G_X, 1): [(G_X, 2)],
    KV_GRAD_C: [(G_X, 2)],
    (FFN, C): [(DRES, C)],
    KV_GRAD_X: [(FFN, C)],
    (PROJ, XF): [(G_X, 1), (G_Z, 3)],
    (FFN, Y): [KV_GRAD_C],
    (DN1, C): [(PROJ, GRAD)],
    (G_Z, 2): [(G_Z, 3)],
    (G_Z, 1): [KV_GRAD_X],
    (PROJ, (Z, 1)): [(FFN, Y), (G_Z, 1)],
    (PROJ, (Z, 2)): [(DN1, Y), (FFN, (Z, 1))],
    (VECTOR, C): [(PROJ, XN)],
    (OUT, X): [(PROJ, XN)],
    (FFN, (Z, 1)): [(FFN, Y)],
    (G_X, 0): [(OUT, X)],
    (OUT, GRAD): [KV_GRAD_C],
    KV_DONE_Y: [(G_Z, 2)],
}


def after(x, *tokens):
    return lax.optimization_barrier((x, *tokens))[0] if tokens else x


def index(x, i, axis=0):
    return lax.dynamic_index_in_dim(x, i, axis, keepdims=False)


def split_columns(weights, n, pieces):
    rows, columns = weights[0].shape
    part, count = columns // n, len(weights)
    flat = [(j, cut) for j in range(n) for cut in pieces[j]]

    def kernel(*refs):
        ins, outs, held = refs[:count], refs[count:-1], refs[-1]
        d = lax.axis_index("dp")
        for i in range(count):
            for t in range(n):
                held[t] = ins[i][:, t * part : (t + 1) * part]
            for out, (j, (low, high)) in zip(outs, flat):
                out[i] = held[d ^ j, low:high]

    outs = pl.pallas_call(
        kernel,
        cost_estimate=CHEAP,
        out_shape=[
            jax.ShapeDtypeStruct((count, high - low, part), BF) for _, (low, high) in flat
        ],
        scratch_shapes=[pltpu.VMEM((n, rows, part), BF)],
        compiler_params=pltpu.CompilerParams(vmem_limit_bytes=48 << 20),
    )(*weights)
    return dict(zip(flat, outs))


def join_columns(blocks):
    n = len(blocks)
    count, rows, part = blocks[0].shape

    def kernel(*refs):
        ins, outs, held = refs[:n], refs[n:-1], refs[-1]
        d = lax.axis_index("dp")
        for i in range(count):
            for j, ref in enumerate(ins):
                held[d ^ j] = ref[i]
            for t in range(n):
                outs[i][:, t * part : (t + 1) * part] = held[t].astype(F32)

    return pl.pallas_call(
        kernel,
        cost_estimate=CHEAP,
        out_shape=[jax.ShapeDtypeStruct((rows, n * part), F32)] * count,
        scratch_shapes=[pltpu.VMEM((n, rows, part), BF)],
        compiler_params=pltpu.CompilerParams(vmem_limit_bytes=48 << 20),
    )(*blocks)


def key_value_slots(w_key, w_value, vectors):
    rows = w_key.shape[0]

    def kernel(key_ref, value_ref, *refs):
        ins, outs = refs[:-2], refs[-2:]
        head = lax.axis_index("mp") // (lax.axis_size("mp") // KVH)
        for i, ref in enumerate((key_ref, value_ref)):
            parts = [ref[:, k * HD : (k + 1) * HD] for k in range(KVH)]
            outs[0][i, :rows] = jnp.where(head == 0, parts[0], parts[1])
            outs[1][i, :rows] = jnp.where(head == 0, parts[1], parts[0])
            for out in outs:
                out[i, rows:] = jnp.zeros((SMALL, HD), BF)
                for j, vector in enumerate(ins):
                    out[i, rows + j : rows + j + 1, : vector.shape[1]] = vector[...]

    return pl.pallas_call(
        kernel, cost_estimate=CHEAP, out_shape=[jax.ShapeDtypeStruct((2, rows + SMALL, HD), BF)] * 2
    )(w_key, w_value, *[v[None] for v in vectors])


def join_rows(own, other, n_dp, n_seq, rows, lens):
    parts = [(a, o, 0) for a, o in own] + [(a, o, 1) for a, o in other]
    width = parts[0][0].shape[2]
    total = sum(len(o) for _, o, _ in parts)
    slots = n_dp * n_seq
    small = parts[0][0].shape[1] - rows

    def kernel(*refs):
        ins, out, vectors = refs[: len(parts)], refs[len(parts)], refs[len(parts) + 1 : -2]
        held, sem = refs[-2:]
        d = lax.axis_index("dp")
        s = lax.axis_index("seq")
        copies = []
        for ref, (_, offsets, side) in zip(ins, parts):
            for i, offset in enumerate(offsets):
                slot = (d ^ offset) * n_seq + (s ^ side)
                start = pl.multiple_of(slot * rows, rows)
                pairs = [(ref.at[i, pl.ds(0, rows)], out.at[pl.ds(start, rows)])]
                if lens:
                    pairs.append((ref.at[i, pl.ds(rows, small)], held.at[slot]))
                for pair in pairs:
                    copies.append(pltpu.make_async_copy(*pair, sem.at[len(copies)]))
        for copy in copies:
            copy.start()
        for copy in copies:
            copy.wait()
        for i, size in enumerate(lens):
            for t in range(slots):
                for k in range(small // SMALL):
                    at = (t * (small // SMALL) + k) * size
                    x = held[t, k * SMALL : (k + 1) * SMALL, :size].astype(F32)
                    vectors[i][:, at : at + size] = x[i : i + 1]

    return pl.pallas_call(
        kernel,
        cost_estimate=CHEAP,
        out_shape=[jax.ShapeDtypeStruct((slots * rows, width), BF)]
        + [jax.ShapeDtypeStruct((1, slots * (small // SMALL) * size), F32) for size in lens],
        in_specs=[pl.BlockSpec(memory_space=pl.ANY)] * len(parts),
        scratch_shapes=[
            pltpu.VMEM((slots, max(small, SMALL), width), BF),
            pltpu.SemaphoreType.DMA((2 * total,)),
        ],
    )(*[a for a, _, _ in parts])


def turn(x, cosine, sine_signed):
    return x * cosine + pltpu.roll(x, HD // 2, 1) * sine_signed


def project(x, vectors, w_q, w_kv, cosine, sine_signed):
    tokens = x.shape[0]
    wide = w_q.shape[1]

    def kernel(x_ref, bq, bk, bv, gain, _, w_ref, wkv_ref, cos_ref, sin_ref, *outs):
        normed, inv_ref, q_ref, kv_ref = outs
        m = lax.axis_index("mp")
        value = x_ref[...].astype(F32)
        inv = inverse_rms(value)
        inv_ref[...] = inv
        norm = (value * inv * gain[...]).astype(BF)
        normed[...] = norm
        proj = dot(norm, w_ref[...])
        cosine, sine = cos_ref[...], sin_ref[...]
        bias = bq[:, pl.ds(pl.multiple_of(m * wide, HD), wide)]
        for j in range(wide // HD):
            cut = slice(j * HD, (j + 1) * HD)
            q_ref[:, cut] = turn(proj[:, cut] + bias[:, cut], cosine, sine).astype(BF)
        head = pl.ds(pl.multiple_of((m // 2) * HD, HD), HD)
        last = dot(norm, wkv_ref[...]) + jnp.where(m % 2 == 0, bk[:, head], bv[:, head])
        kv_ref[...] = jnp.where(m % 2 == 0, turn(last, cosine, sine), last).astype(BF)

    return pl.pallas_call(
        kernel,
        cost_estimate=CHEAP,
        out_shape=[
            jax.ShapeDtypeStruct(x.shape, BF),
            jax.ShapeDtypeStruct((tokens, 1), F32),
            jax.ShapeDtypeStruct((tokens, wide), BF),
            jax.ShapeDtypeStruct((tokens, HD), BF),
        ],
    )(x, *vectors, w_q, w_kv, cosine, sine_signed)


def attend(query, seen, other, mask, out_t, quarter):
    tokens, wide = query.shape
    heads = wide // HD
    width = out_t.shape[0]

    def kernel(q_ref, seen_ref, other_ref, mask_ref, o_ref, att, log_ref, near, away, held):
        c = lax.axis_index("mp") % 2
        keys = jnp.where(c == 0, seen_ref[...], other_ref[...])
        vals = jnp.where(c == 0, other_ref[...], seen_ref[...])
        for j in range(heads):
            cut = slice(j * HD, (j + 1) * HD)
            scores = dot_nt(q_ref[:, cut], keys) * HD ** (-0.5) + mask_ref[...]
            top = jnp.max(scores, axis=-1, keepdims=True)
            total = jnp.sum(jnp.exp(scores - top), axis=-1, keepdims=True)
            log_total = top + jnp.log(total)
            log_ref[:, j : j + 1] = log_total
            att[:, cut] = dot(jnp.exp(scores - log_total).astype(BF), vals).astype(BF)
        held[...] = dot_nt(att[...], o_ref[...])
        for i in range(2):
            rows = pl.ds(pl.multiple_of((2 * i + c) * quarter, quarter), quarter)
            near[i] = held[rows]
            rows = pl.ds(pl.multiple_of((2 * i + 1 - c) * quarter, quarter), quarter)
            away[i] = held[rows].astype(BF)

    return pl.pallas_call(
        kernel,
        cost_estimate=CHEAP,
        out_shape=[
            jax.ShapeDtypeStruct((tokens, wide), BF),
            jax.ShapeDtypeStruct((tokens, heads), F32),
            jax.ShapeDtypeStruct((2, quarter, width), F32),
            jax.ShapeDtypeStruct((2, quarter, width), BF),
        ],
        scratch_shapes=[pltpu.VMEM((tokens, width), F32)],
    )(query, seen, other, mask, out_t)


def feed_rows(n2, cot, gate_ref, up_ref, down_ref, outs, waits):
    act, diff_gate_ref, diff_up_ref, dn = outs
    size = min(256, n2.shape[0])
    for i in range(n2.shape[0] // size):
        rows = slice(i * size, (i + 1) * size)
        if i == 0:
            waits[0]()
        gate_proj = dot(n2[rows], gate_ref[...])
        if i == 0:
            waits[1]()
        up_proj = dot(n2[rows], up_ref[...])
        if i == 0:
            waits[2]()
        diff_hidden = dot(cot[rows], down_ref[...])
        sigmoid_gate = 1.0 / (1.0 + jnp.exp(-gate_proj))
        silu_gate = gate_proj * sigmoid_gate
        act[rows] = (silu_gate * up_proj).astype(BF)
        diff_gate = (
            diff_hidden * up_proj * sigmoid_gate * (1.0 + gate_proj * (1.0 - sigmoid_gate))
        ).astype(BF)
        diff_up = (diff_hidden * silu_gate).astype(BF)
        diff_gate_ref[rows] = diff_gate
        diff_up_ref[rows] = diff_up
        dn[rows] = (dot_nt(diff_gate, gate_ref[...]) + dot_nt(diff_up, up_ref[...])).astype(dn.dtype)


def feed_shapes(n2, part, kind):
    shape = jax.ShapeDtypeStruct((n2.shape[0], part), BF)
    return [shape] * 3 + [jax.ShapeDtypeStruct(n2.shape, kind)]


def feed_limit(n2, part):
    part = -(-part // HD) * HD
    return min(60 << 20, (10 << 20) + 8 * n2.size + 12 * sum(n2.shape) * part)


def feed_first(n2, cot, blocks, rows, n_dp, n_seq):
    keys = list(blocks)
    part = blocks[keys[0]].shape[2]
    full = n_dp * n_seq * rows

    def kernel(n2_ref, cot_ref, *refs):
        ins, copies_out, outs = refs[: len(keys)], refs[len(keys) :][:3], refs[len(keys) + 3 :][:4]
        weights, sem = refs[-4:-1], refs[-1]
        d = lax.axis_index("dp")
        s = lax.axis_index("seq")
        back = [
            pltpu.make_async_copy(weights[w], copies_out[w], sem.at[w]) for w in range(3)
        ]

        def place(which):
            for ref, (side, j, (low, high)) in zip(ins, keys):
                size = high - low
                start = ((d ^ j) * n_seq + (s ^ side)) * rows + low
                weights[which][pl.ds(pl.multiple_of(start, size), size)] = ref[which]
            back[which].start()

        waits = [lambda w=w: place(w) for w in range(3)]
        feed_rows(n2_ref, cot_ref, *weights, outs, waits)
        for copy in back:
            copy.wait()

    whole = pl.BlockSpec(memory_space=pltpu.VMEM)
    return pl.pallas_call(
        kernel,
        cost_estimate=CHEAP,
        out_shape=[pltpu.HBM((full, part), BF)] * 3 + feed_shapes(n2, part, BF),
        out_specs=[pl.BlockSpec(memory_space=pltpu.HBM)] * 3 + [whole] * 4,
        scratch_shapes=[pltpu.VMEM((full, part), BF)] * 3
        + [pltpu.SemaphoreType.DMA((3,))],
        compiler_params=pltpu.CompilerParams(vmem_limit_bytes=feed_limit(n2, part)),
    )(n2, cot, *blocks.values())


def feed_second(n2, cot, gate, up, down):
    part = gate.shape[1]

    def kernel(n2_ref, cot_ref, gate_ref, up_ref, down_ref, *outs):
        feed_rows(n2_ref, cot_ref, gate_ref, up_ref, down_ref, outs, [lambda: None] * 3)

    return pl.pallas_call(
        kernel,
        cost_estimate=CHEAP,
        out_shape=feed_shapes(n2, part, F32),
        compiler_params=pltpu.CompilerParams(vmem_limit_bytes=feed_limit(n2, part)),
    )(n2, cot, gate, up, down)


def weight_grads(rows, which, diffs, n_dp, n_seq, far):
    count, half, n = len(diffs), n_dp // 2, 2 * len(rows)
    wide = rows[0][0].shape[1] // n_dp
    size, width = wide // n_seq, diffs[0][0].shape[1]
    operands = [a for pair in rows for a in pair] + [a for pair in diffs for a in pair]

    def kernel(*refs):
        ins, outs, held = refs[: len(operands)], refs[len(operands) : -1], refs[-1]
        d = lax.axis_index("dp")
        s = lax.axis_index("seq")
        upper = (d // half) ^ int(far)

        def columns(ref, t):
            if wide % HD == 0:
                start = upper * (half * wide) + t * wide
                return ref[:, pl.ds(pl.multiple_of(start, HD), wide)]
            low = ref[:, t * wide : (t + 1) * wide]
            high = ref[:, (half + t) * wide : (half + t + 1) * wide]
            return jnp.where(upper == 0, low, high)

        for i in range(count):
            for t in range(half):
                k = 2 * which[i]
                x = dot_tn(columns(ins[k], t), ins[n + 2 * i][...])
                x = x + dot_tn(columns(ins[k + 1], t), ins[n + 2 * i + 1][...])
                x = x.astype(BF)
                held[t, 0] = x[:size]
                held[t, 1] = x[size:]
            for j in range(half):
                outs[j][i] = held[(d % half) ^ j, s]
                outs[half + j][i] = held[(d % half) ^ j, 1 - s]

    total = sum(a.size for a in operands)
    need = (6 << 20) + (2 if total < 8 << 20 else 4) * total
    outs = pl.pallas_call(
        kernel,
        cost_estimate=CHEAP,
        out_shape=[jax.ShapeDtypeStruct((count, size, width), BF)] * n_dp,
        scratch_shapes=[pltpu.VMEM((half, n_seq, size, width), BF)],
        compiler_params=pltpu.CompilerParams(vmem_limit_bytes=min(60 << 20, need)),
    )(*operands)
    return outs[:half], outs[half:]


def token_grads(rows, diff, n_dp, n_seq, groups):
    wide = rows.shape[1] // n_dp
    size, width = wide // n_seq, diff.shape[1]

    def kernel(rows_ref, diff_ref, *refs):
        outs, held = refs[:-1], refs[-1]
        d = lax.axis_index("dp")
        s = lax.axis_index("seq")
        for t in range(n_dp):
            x = dot_tn(rows_ref[:, t * wide : (t + 1) * wide], diff_ref[...]).astype(BF)
            held[t, 0] = x[:size]
            held[t, 1] = x[size:]
        for side in range(2):
            for out, group in zip(outs[side * len(groups) :], groups):
                for i, offset in enumerate(group):
                    out[i] = held[d ^ offset, s ^ side]

    outs = pl.pallas_call(
        kernel,
        cost_estimate=CHEAP,
        out_shape=[jax.ShapeDtypeStruct((len(g), size, width), BF) for g in groups] * 2,
        scratch_shapes=[pltpu.VMEM((n_dp, n_seq, size, width), BF)],
    )(rows, diff)
    return outs[: len(groups)], outs[len(groups) :]


def solution(mesh):
    n_dp = mesh.shape["dp"]
    n_seq = mesh.shape["seq"]
    n_mp = mesh.shape["mp"]
    bits = [1 << i for i in reversed(range(n_dp.bit_length() - 1))]

    def on_device(
        inputs,
        cotangent,
        segments,
        positions,
        w_query,
        w_key,
        w_value,
        bias_query,
        bias_key,
        bias_value,
        w_out,
        gain_attn,
        gain_ffn,
        w_gate,
        w_up,
        w_down,
    ):
        d = lax.axis_index("dp")
        s = lax.axis_index("seq")
        m = lax.axis_index("mp")
        y, c = m // 2, m % 2
        tokens = inputs.shape[0]
        quarter = tokens // n_mp
        score_scale = HD ** (-0.5)
        wide = w_query.shape[1]
        heads_local = wide // HD
        rows_kv = w_key.shape[0]

        values, makers = {}, {}

        def get(name):
            if name not in values:
                values[name] = makers[name]()
            return values[name]

        def task(name):
            def add(maker):
                makers[name] = maker

            return add

        def tied(name, x):
            tokens = [jax.tree.leaves(get(o))[0] for o in AFTER.get(name, ()) if o in makers]
            return after(x, *tokens)

        links = {X: ("seq", [(0, 1), (1, 0)]), X01: ("seq", [(0, 1)]), X10: ("seq", [(1, 0)])}
        for k in range(1, n_dp):
            links[(Z, k)] = ("dp", [(j, j ^ k) for j in range(n_dp)])
        for k, name in ((1, C), (2, Y)):
            links[name] = ("mp", [(j, j ^ k) for j in range(n_mp)])

        def move(name, link, maker):
            makers[name] = lambda: lax.ppermute(tied(name, maker()), *links[link])

        def of(name):
            return lambda: get(name)

        def gather(name, maker, size, lens, split):
            makers[(name, PAY)] = lambda: maker()[None]
            pay, offsets = (name, PAY), [0]
            for k in bits[:-1]:
                recv = (name, (Z, k))
                move(recv, (Z, k), of(pay))
                makers[(recv, PAY)] = lambda a=pay, b=recv: jnp.concatenate([get(a), get(b)])
                pay, offsets = (recv, PAY), offsets + [o ^ k for o in offsets]
            k = bits[-1]
            recv = (name, (Z, k))
            move(recv, (Z, k), of(pay))
            there = [o ^ k for o in offsets]
            if split:
                move((name, XA), X, of(pay))
                move((name, XB), X, of(recv))
                own = lambda: [(get(pay), offsets), (get(recv), there)]
                other = lambda: [(get((name, XA)), offsets), (get((name, XB)), there)]
            else:
                makers[(name, BOTH)] = lambda: jnp.concatenate([get(pay), get(recv)])
                move((name, X), X, of((name, BOTH)))
                own = lambda: [(get((name, BOTH)), offsets + there)]
                other = lambda: [(get((name, X)), offsets + there)]
            makers[name] = lambda: join_rows(own(), other(), n_dp, n_seq, size, lens)

        w_rows = w_gate.shape[0]
        whole_cut = [(0, w_rows)]
        third = w_rows // 3
        third_cuts = [(i * third, (i + 1) * third) for i in range(3)]
        pieces = [whole_cut if k < n_dp // 2 else third_cuts for k in range(n_dp)]
        tails = [(k, cut, (k, i)) for k in range(n_dp) for i, cut in enumerate(pieces[k])]
        makers[W_PREP] = lambda: split_columns(
            [tied(W_PREP, w_gate), w_up, w_down.T], n_dp, pieces
        )
        for k, cut, tail in tails:
            if k:
                move((W_Z, tail), (Z, k), lambda k=k, cut=cut: get(W_PREP)[k, cut])
            else:
                makers[(W_Z, tail)] = lambda cut=cut: get(W_PREP)[0, cut]
            move((W_X, tail), X, of((W_Z, tail)))

        def rows_gather(name, maker):
            makers[(name, PAY)] = maker
            pay = (name, PAY)
            for k in bits[:-1]:
                recv = (name, (Z, k))
                move(recv, (Z, k), of(pay))
                makers[(recv, PAY)] = lambda a=pay, b=recv: jnp.concatenate([get(a), get(b)])
                pay = (recv, PAY)
            recv = (name, (Z, bits[-1]))
            move(recv, (Z, bits[-1]), of(pay))
            move((name, YA), Y, of(pay))
            move((name, YB), Y, of(recv))
            makers[(name, OWN)] = lambda: jnp.concatenate(
                [get(pay), get(recv), get((name, YA)), get((name, YB))]
            )
            move((name, C), C, of((name, OWN)))

        def rows_sum(name, split):
            move((name, C), C, of((name, AWAY)))
            last = (name, (Z, bits[-1]))

            def part(i):
                size = get((name, OWN)).shape[0] // 4
                cut = slice(i * size, (i + 1) * size)
                return get((name, OWN))[cut] + get((name, C))[cut].astype(F32)

            for i in range(4):
                makers[(name, PART, i)] = lambda i=i: part(i)
            if split:
                move((name, YB), Y, lambda: get((name, PART, 3)).astype(BF))
                move((name, YA), Y, lambda: get((name, PART, 2)).astype(BF))
            else:

                def parts():
                    return jnp.concatenate([get((name, PART, 2)), get((name, PART, 3))]).astype(BF)

                move((name, Y), Y, parts)
                makers[(name, YA)] = lambda: get((name, Y))[: get((name, PART, 2)).shape[0]]
                makers[(name, YB)] = lambda: get((name, Y))[get((name, PART, 2)).shape[0] :]
            move(
                last,
                (Z, bits[-1]),
                lambda: (get((name, PART, 1)) + get((name, YB)).astype(F32)).astype(BF),
            )
            makers[(name, LEFT, 0)] = (
                lambda: get((name, PART, 0)) + get((name, YA)).astype(F32) + get(last).astype(F32)
            )
            left = (name, LEFT, 0)
            for i, k in enumerate(reversed(bits[:-1])):
                recv = (name, (Z, k))

                def far(left=left):
                    return get(left)[get(left).shape[0] // 2 :].astype(BF)

                def near(left=left, recv=recv):
                    return get(left)[: get(left).shape[0] // 2] + get(recv).astype(F32)

                move(recv, (Z, k), far)
                left = (name, LEFT, i + 1)
                makers[left] = near
            makers[name] = of(left)

        def weight_grad_ways(name, far):
            own, away = get(HIDDEN_OWN), get(HIDDEN_AWAY)
            n2 = [tied(name, get((N2, OWN))), get((N2, C))]
            cot = [get((COT, OWN)), get((COT, C))]
            return weight_grads(
                [n2, cot],
                [0, 0, 1],
                [[own[1], away[1]], [own[2], away[2]], [own[0], away[0]]],
                n_dp,
                n_seq,
                far,
            )

        makers[GRADS_FAR] = lambda: weight_grad_ways(GRADS_FAR, True)
        makers[GRADS_NEAR] = lambda: weight_grad_ways(GRADS_NEAR, False)

        def grad_piece(k, side):
            return get(GRADS_NEAR if k < n_dp // 2 else GRADS_FAR)[side][k % (n_dp // 2)]

        for k in range(n_dp):
            move((G_X, k), X, lambda k=k: grad_piece(k, 1))
        for k in range(n_dp):

            def summed(k=k):
                own = tied((G_SUM, k), grad_piece(k, 0)).astype(F32)
                return (own + get((G_X, k)).astype(F32)).astype(BF)

            makers[(G_SUM, k)] = summed
            if k:
                move((G_Z, k), (Z, k), of((G_SUM, k)))
            else:
                makers[(G_Z, k)] = of((G_SUM, k))
        makers[GRADS_DONE] = lambda: join_columns(
            [get((G_Z, k)) for k in range(n_dp)]
        )

        def gather_grad(name, rows, diff, split):
            near = [0]
            for k in bits[:-1]:
                near = near + [o ^ k for o in near]
            far = [o ^ bits[-1] for o in near]
            n_near = len(near)
            groups = [near, far] if split else [near + far]
            makers[(name, GRAD)] = lambda: token_grads(rows(), diff(), n_dp, n_seq, groups)
            if split:
                move((name, XF), X, lambda: get((name, GRAD))[1][1])
                move((name, XN), X, lambda: get((name, GRAD))[1][0])
                own = lambda i: get((name, GRAD))[0][i]
            else:
                move((name, X), X, lambda: get((name, GRAD))[1][0])
                makers[(name, XN)] = lambda: get((name, X))[:n_near]
                makers[(name, XF)] = lambda: get((name, X))[n_near:]
                own = lambda i: get((name, GRAD))[0][0][i * n_near : (i + 1) * n_near]

            def both(i, recv):
                return own(i).astype(F32) + get(recv).astype(F32)

            last = (name, (Z, bits[-1]))
            move(last, (Z, bits[-1]), lambda: both(1, (name, XF)).astype(BF))
            makers[(name, LEFT, 0)] = lambda: both(0, (name, XN)) + get(last).astype(F32)
            left = (name, LEFT, 0)
            for i, k in enumerate(reversed(bits[:-1])):
                recv = (name, (Z, k))

                def far_half(left=left):
                    return get(left)[get(left).shape[0] // 2 :].astype(BF)

                def near_half(left=left, recv=recv):
                    return get(left)[: get(left).shape[0] // 2] + get(recv).astype(F32)

                move(recv, (Z, k), far_half)
                left = (name, LEFT, i + 1)
                makers[left] = near_half
            makers[(name, DONE)] = lambda: get(left)[0]

        def mp_gather(name, maker):
            move((name, Y), Y, maker)

            def pair():
                a, b = maker(), get((name, Y))
                return jnp.where(y == 0, jnp.stack([a, b]), jnp.stack([b, a]))

            makers[(name, PAIR)] = pair
            move((name, C), C, of((name, PAIR)))

            def whole():
                a, b = get((name, PAIR)), get((name, C))
                both = jnp.where(c == 0, jnp.stack([a, b], axis=1), jnp.stack([b, a], axis=1))
                return both.reshape(-1, both.shape[-1])

            makers[name] = whole

        def mp_sum(name, maker):
            def blocks():
                x = maker()
                return x.reshape(2, 2, -1, x.shape[-1])

            makers[(name, BLOCKS)] = blocks
            move((name, C), C, lambda: index(get((name, BLOCKS)), 1 - c, 1).astype(BF))
            makers[(name, HALF)] = lambda: index(get((name, BLOCKS)), c, 1) + get(
                (name, C)
            ).astype(F32)
            move((name, Y), Y, lambda: index(get((name, HALF)), 1 - y).astype(BF))
            makers[name] = lambda: index(get((name, HALF)), y) + get((name, Y)).astype(F32)

        gather(QUERY, lambda: w_query, w_query.shape[0], [], True)
        gather(O_ALL, lambda: tied(O_ALL, w_out).T, w_query.shape[0], [], False)
        makers[OUT_FULL] = lambda: get(O_ALL)[0]

        vectors = (bias_query, bias_key, bias_value, gain_attn, gain_ffn)

        makers[KV_SLOTS] = lambda: key_value_slots(w_key, w_value, vectors)
        move((KV, Y), Y, lambda: get(KV_SLOTS)[1])

        @task(KV_PAIRS)
        def kv_pairs():
            return jnp.stack([get(KV_SLOTS)[0], get((KV, Y))])

        move((KV, C), C, lambda: index(get(KV_PAIRS), 1 - c, 1))

        @task(KV_ROWS)
        def kv_rows():
            own, got = index(get(KV_PAIRS), c, 1), get((KV, C))
            by_core = jnp.where(
                c == 0, jnp.stack([own, got], axis=1), jnp.stack([got, own], axis=1)
            )
            whole = jnp.where(y == 0, by_core, by_core[::-1])
            parts = [whole[:, :, :rows_kv], whole[:, :, rows_kv:]]
            return jnp.concatenate([x.reshape(-1, HD) for x in parts])

        gather(
            KV, of(KV_ROWS), n_mp * rows_kv, [v.shape[0] for v in vectors], False
        )

        @task(IN_FLOAT)
        def in_float():
            return tied(INPUTS, inputs).astype(F32)

        @task(ROPE)
        def rope():
            cosine, sine_table = rope_tables(tied(POSITIONS, positions))
            first = jnp.arange(HD) < HD // 2
            return cosine, jnp.where(first, -sine_table, sine_table)

        @task(PROJECTED)
        def projected():
            weights, *small = get(KV)
            x = tied(PROJECT, inputs)
            return project(x, small, get(QUERY)[0], weights, *get(ROPE))

        makers[NORMED_ONE] = lambda: get(PROJECTED)[0]
        makers[INV_ONE] = lambda: get(PROJECTED)[1]
        makers[QUERY_ROT] = lambda: get(PROJECTED)[2]
        makers[KV_ROT] = lambda: tied(KV_ROT, get(PROJECTED)[3])

        move(KV_ACT_X, X01, of(KV_ROT))

        @task(KV_SEEN)
        def kv_seen():
            return jnp.concatenate([get(KV_ACT_X), get(KV_ROT)], axis=0)

        move(KV_ACT_C, C, of(KV_SEEN))

        @task(MASK_TABLE)
        def mask_table():
            where = tied(MASK, segments)
            seg_before = where[:tokens]
            seg_own = lax.dynamic_slice_in_dim(where, s * tokens, tokens, 0)
            order = jnp.arange(tokens, dtype=jnp.int32)
            before = (seg_own[:, None] == seg_before[None, :]) & (s > 0)
            own = (seg_own[:, None] == seg_own[None, :]) & (order[None, :] <= order[:, None])
            return jnp.where(jnp.concatenate([before, own], axis=1), 0.0, NEG_BIG)

        @task(HEADS)
        def heads():
            return attend(
                get(QUERY_ROT),
                get(KV_SEEN),
                tied(HEADS, get(KV_ACT_C)),
                get(MASK_TABLE),
                get(OUT_FULL),
                quarter,
            )

        makers[ATTENDED] = lambda: get(HEADS)[0]

        move(BRANCH_C, C, lambda: get(HEADS)[3])
        makers[BRANCH_HALF] = lambda: get(HEADS)[2] + get(BRANCH_C).astype(F32)
        move(BRANCH_Y, Y, lambda: index(get(BRANCH_HALF), 1 - y).astype(BF))
        makers[BRANCH] = lambda: index(get(BRANCH_HALF), y) + get(BRANCH_Y).astype(F32)

        @task(IN_QUARTER)
        def in_quarter():
            return lax.dynamic_slice_in_dim(get(IN_FLOAT), m * quarter, quarter, 0)

        @task(HIDDEN_RES)
        def hidden_res():
            return get(IN_QUARTER) + get(BRANCH)

        @task(INV_TWO)
        def inv_two():
            return inverse_rms(get(HIDDEN_RES))

        @task(NORMED_TWO)
        def normed_two():
            return tied(
                NORMED_TWO, (get(HIDDEN_RES) * get(INV_TWO) * get(KV)[5]).astype(BF)
            )

        @task(COT_QUARTER)
        def cot_quarter():
            return lax.dynamic_slice_in_dim(cotangent, m * quarter, quarter, 0)

        rows_gather(N2, of(NORMED_TWO))
        rows_gather(COT, of(COT_QUARTER))

        @task(FEED_AWAY)
        def feed_away():
            blocks = {(0, k, cut): get((W_Z, tail)) for k, cut, tail in tails}
            blocks.update({(1, k, cut): get((W_X, tail)) for k, cut, tail in tails})
            return feed_first(
                tied(FEED_AWAY, get((N2, C))), get((COT, C)), blocks, w_rows, n_dp, n_seq
            )

        @task(FEED_OWN)
        def feed_own():
            weights = get(FEED_AWAY)[:3]
            return feed_second(tied(FEED_OWN, get((N2, OWN))), get((COT, OWN)), *weights)

        makers[HIDDEN_AWAY] = lambda: get(FEED_AWAY)[3:6]
        makers[HIDDEN_OWN] = lambda: get(FEED_OWN)[:3]
        makers[(DN, AWAY)] = lambda: get(FEED_AWAY)[6]
        makers[(DN, OWN)] = lambda: get(FEED_OWN)[3]
        makers[(FFN, OWN)] = lambda: dot_nt(
            tied((FFN, OWN), get(HIDDEN_OWN)[0]), get(FEED_AWAY)[2]
        )
        makers[(FFN, AWAY)] = lambda: dot_nt(
            tied((FFN, AWAY), get(HIDDEN_AWAY)[0]), get(FEED_AWAY)[2]
        ).astype(BF)
        rows_sum(DN, True)

        rows_sum(FFN, False)

        @task(DIFF_RES)
        def diff_res():
            return get(COT_QUARTER).astype(F32) + norm_backward(
                get(DN), get(HIDDEN_RES), get(INV_TWO), get(KV)[5]
            )

        mp_gather(DRES, lambda: get(DIFF_RES).astype(BF))

        @task(HEADS_BACK)
        def heads_back():
            seen, other = get(KV_SEEN), get(KV_ACT_C)
            keys, vals = jnp.where(c == 0, seen, other), jnp.where(c == 0, other, seen)
            queries, logs = get(QUERY_ROT), get(HEADS)[1]
            diff_attended = tied(HEADS_BACK, dot(get(DRES), get(OUT_FULL)).astype(BF))
            return [
                head_backward(
                    queries[:, j * HD : (j + 1) * HD],
                    keys,
                    vals,
                    get(MASK_TABLE),
                    score_scale,
                    logs[:, j : j + 1],
                    get(ATTENDED)[:, j * HD : (j + 1) * HD],
                    diff_attended[:, j * HD : (j + 1) * HD],
                )
                for j in range(heads_local)
            ]

        @task(KV_SUMS)
        def kv_sums():
            return [sum(head[i] for head in get(HEADS_BACK)) for i in (1, 2)]

        move(KV_GRAD_C, C, lambda: jnp.where(c == 0, *reversed(get(KV_SUMS))))

        @task(KV_SUM)
        def kv_sum():
            return jnp.where(c == 0, *get(KV_SUMS)) + get(KV_GRAD_C)

        move(KV_GRAD_X, X10, lambda: get(KV_SUM)[:tokens])

        def turn_back(x):
            cosine, sine_signed = get(ROPE)
            return x * cosine - jnp.roll(x, HD // 2, axis=1) * sine_signed

        @task(KV_PRE)
        def kv_pre():
            mine = get(KV_SUM)[tokens:] + get(KV_GRAD_X)
            return jnp.where(c == 0, turn_back(mine), mine)

        @task(QUERY_PRE)
        def query_pre():
            return jnp.concatenate([turn_back(head[0]) for head in get(HEADS_BACK)], axis=1)

        @task(QKV_CAST)
        def qkv_cast():
            return jnp.concatenate([get(QUERY_PRE), get(KV_PRE)], axis=1).astype(BF)

        gather_grad(PROJ, of(NORMED_ONE), of(QKV_CAST), True)
        gather_grad(OUT, lambda: tied((OUT, GRAD), get(DRES)), of(ATTENDED), False)

        @task(DIFF_NORMED)
        def diff_normed():
            cast = get(QKV_CAST)
            return dot_nt(cast[:, :wide], get(QUERY)[0]) + dot_nt(cast[:, wide:], get(KV)[0])

        mp_sum(DN1, of(DIFF_NORMED))

        @task((KV, DONE))
        def kv_done():
            return get((PROJ, DONE))[:, wide:].reshape(2, 2, rows_kv, HD).astype(BF)

        move(KV_DONE_Y, Y, lambda: index(get((KV, DONE)), 1 - y))

        @task(KV_DONE_HEADS)
        def kv_done_heads():
            mine, got = index(get((KV, DONE)), y), get(KV_DONE_Y)
            return jnp.where(y == 0, jnp.stack([mine, got]), jnp.stack([got, mine]))

        move(KV_DONE_C, C, lambda: index(get(KV_DONE_HEADS), 1 - c, 1))

        @task(KV_GRADS)
        def kv_grads():
            mine, got = index(get(KV_DONE_HEADS), c, 1), get(KV_DONE_C)
            return [
                jnp.where(c == 0, a, b)
                .transpose(1, 0, 2)
                .reshape(rows_kv, KVH * HD)
                .astype(F32)
                for a, b in ((mine, got), (got, mine))
            ]

        @task(INV_QUARTER)
        def inv_quarter():
            return lax.dynamic_slice_in_dim(get(INV_ONE), m * quarter, quarter, 0)

        @task(INPUT_DIFF)
        def input_diff():
            return get(DIFF_RES) + norm_backward(
                get(DN1), get(IN_QUARTER), get(INV_QUARTER), get(KV)[4]
            )

        mp_gather(
            RESULTS,
            lambda: jnp.concatenate(
                [get(HIDDEN_RES) + get(FFN), get(INPUT_DIFF)], axis=1
            ).astype(BF),
        )

        @task(VECTOR)
        def vector():
            grad_gain_ffn = jnp.sum(get(DN) * get(HIDDEN_RES) * get(INV_TWO), axis=0)
            grad_gain_attn = jnp.sum(get(DN1) * get(IN_QUARTER) * get(INV_QUARTER), axis=0)
            grad_bq = jnp.sum(get(QUERY_PRE), axis=0)
            grad_bkv = jnp.sum(get(KV_PRE), axis=0)
            zeros_kv = jnp.zeros((2, KVH, HD), F32)
            return jnp.concatenate(
                [
                    lax.dynamic_update_slice_in_dim(
                        jnp.zeros((H * HD,), F32), grad_bq, m * wide, 0
                    ),
                    grad_gain_attn,
                    grad_gain_ffn,
                    lax.dynamic_update_slice(zeros_kv, grad_bkv[None, None], (c, y, 0)).reshape(-1),
                ]
            ).reshape(-1, HD)

        total = VECTOR
        for link in [C, Y, X] + [(Z, k) for k in bits]:
            move((VECTOR, link), link, of(total))
            makers[(TOTAL, link)] = lambda a=total, b=(VECTOR, link): get(a) + get(b)
            total = (TOTAL, link)

        makers[SUMS] = lambda: get(total).reshape(-1)
        device = (d * n_seq + s) * n_mp + m

        def own(start, length):
            width = length // (n_dp * n_seq * n_mp)
            return lax.dynamic_slice_in_dim(
                get(SUMS)[start : start + length], device * width, width, 0
            )

        return (
            get(RESULTS)[:, :D].astype(F32),
            get(RESULTS)[:, D:].astype(F32),
            get((PROJ, DONE))[:, :wide],
            get(KV_GRADS)[0],
            get(KV_GRADS)[1],
            own(0, H * HD),
            get(SUMS)[3 * D : 3 * D + KVH * HD],
            own(3 * D + KVH * HD, KVH * HD),
            get((OUT, DONE)).T,
            own(D, D),
            own(2 * D, D),
            get(GRADS_DONE)[0],
            get(GRADS_DONE)[1],
            get(GRADS_DONE)[2].T,
        )

    in_specs = (
        P(("dp", "seq"), None),
        P(("dp", "seq"), None),
        P("dp"),
        P(("dp", "seq")),
        P(("dp", "seq"), "mp"),
        P(("dp", "seq", "mp"), None),
        P(("dp", "seq", "mp"), None),
        P(("dp", "seq", "mp")),
        P(("dp", "seq", "mp")),
        P(("dp", "seq", "mp")),
        P("mp", ("dp", "seq")),
        P(("dp", "seq", "mp")),
        P(("dp", "seq", "mp")),
        P(("dp", "seq"), "mp"),
        P(("dp", "seq"), "mp"),
        P("mp", ("dp", "seq")),
    )
    out_specs = (
        P(("dp", "seq"), None),
        P(("dp", "seq"), None),
        P(("dp", "seq"), "mp"),
        P(("dp", "seq", "mp"), None),
        P(("dp", "seq", "mp"), None),
        P(("dp", "seq", "mp")),
        P(),
        P(("dp", "seq", "mp")),
        P("mp", ("dp", "seq")),
        P(("dp", "seq", "mp")),
        P(("dp", "seq", "mp")),
        P(("dp", "seq"), "mp"),
        P(("dp", "seq"), "mp"),
        P("mp", ("dp", "seq")),
    )
    return jax.shard_map(
        on_device, mesh=mesh, in_specs=in_specs, out_specs=out_specs, check_vma=False
    )
```

```python
import math

import jax
import jax.numpy as jnp
from jax import lax
from jax.experimental import pallas as pl
from jax.experimental.pallas import tpu as pltpu
from jax.sharding import PartitionSpec as P

D = 1536
H = 12
KVH = 2
HD = 128

EPSILON = 1e-06
ROPE_BASE = 1000000.0
NEG_BIG = -1e30
SMALL = 16
CHEAP = pl.CostEstimate(flops=0, bytes_accessed=0, transcendentals=0)
BF = jnp.bfloat16
F32 = jnp.float32


def dot(a, b):
    return jnp.dot(a, b, preferred_element_type=F32)


def dot_nt(a, b):
    return lax.dot_general(a, b, (((1,), (1,)), ((), ())), preferred_element_type=F32)


def dot_tn(a, b):
    return lax.dot_general(a, b, (((0,), (0,)), ((), ())), preferred_element_type=F32)


def inverse_rms(values):
    return lax.rsqrt(jnp.mean(values * values, axis=-1, keepdims=True) + EPSILON)


def norm_backward(upstream, values, inv_scale, gain_vec):
    scaled = upstream * gain_vec
    return inv_scale * scaled - values * (inv_scale * inv_scale * inv_scale) * jnp.mean(
        scaled * values, axis=-1, keepdims=True
    )


def rope_tables(positions):
    steps_half = jnp.arange(0, HD, 2).astype(F32)
    frequency = jnp.exp(steps_half * (-math.log(ROPE_BASE) / HD))
    angles = positions.astype(F32)[:, None] * frequency[None, :]
    angles = jnp.concatenate([angles, angles], axis=-1)
    return (jnp.cos(angles), jnp.sin(angles))


def head_backward(
    query_rows, key_rows, value_rows, mask_table, score_scale, log_total, attended, diff_attended
):
    scores = dot_nt(query_rows, key_rows) * score_scale + mask_table
    prob_full = jnp.exp(scores - log_total)
    prob_cast = prob_full.astype(BF)
    value_part = dot_tn(prob_cast, diff_attended)
    diff_probs = dot_nt(diff_attended, value_rows)
    row_delta = jnp.sum(
        diff_attended.astype(F32) * attended.astype(F32), axis=-1, keepdims=True
    )
    diff_scores = (prob_full * (diff_probs - row_delta) * score_scale).astype(BF)
    diff_query = dot(diff_scores, key_rows)
    key_part = dot_tn(diff_scores, query_rows)
    return (diff_query, key_part, value_part)


(
    ATTENDED,
    AWAY,
    BLOCKS,
    BOTH,
    BRANCH,
    BRANCH_C,
    BRANCH_HALF,
    BRANCH_Y,
    C,
    COT,
    COT_QUARTER,
    DIFF_NORMED,
    DIFF_RES,
    DN,
    DN1,
    DONE,
    DRES,
    FEED_AWAY,
    FEED_OWN,
    FFN,
    GRAD,
    GRADS_DONE,
    GRADS_FAR,
    GRADS_NEAR,
    G_SUM,
    G_X,
    G_Z,
    HALF,
    HEADS,
    HEADS_BACK,
    HIDDEN_AWAY,
    HIDDEN_OWN,
    HIDDEN_RES,
    INPUTS,
    INPUT_DIFF,
    INV_ONE,
    INV_QUARTER,
    INV_TWO,
    IN_FLOAT,
    IN_QUARTER,
    KV,
    KV_ACT_C,
    KV_ACT_X,
    KV_DONE_C,
    KV_DONE_HEADS,
    KV_DONE_Y,
    KV_GRADS,
    KV_GRAD_C,
    KV_GRAD_X,
    KV_PAIRS,
    KV_PRE,
    KV_ROT,
    KV_ROWS,
    KV_SEEN,
    KV_SLOTS,
    KV_SUM,
    KV_SUMS,
    LEFT,
    MASK,
    MASK_TABLE,
    N2,
    NORMED_ONE,
    NORMED_TWO,
    OUT,
    OUT_FULL,
    OWN,
    O_ALL,
    PAIR,
    PART,
    PAY,
    POSITIONS,
    PROJ,
    PROJECT,
    PROJECTED,
    QKV_CAST,
    QUERY,
    QUERY_PRE,
    QUERY_ROT,
    RESULTS,
    ROPE,
    SUMS,
    TOTAL,
    VECTOR,
    W_PREP,
    W_X,
    W_Z,
    X,
    X01,
    X10,
    XA,
    XB,
    XF,
    XN,
    Y,
    YA,
    YB,
    Z,
) = range(97)

AFTER = {
    (W_X, (0, 0)): [(O_ALL, X)],
    (O_ALL, (Z, 2)): [(QUERY, (Z, 2))],
    (QUERY, XB): [(O_ALL, (Z, 2))],
    (W_Z, (2, 0)): [(QUERY, (Z, 1))],
    (O_ALL, (Z, 1)): [(QUERY, (Z, 1))],
    PROJECT: [(O_ALL, (Z, 1))],
    (COT, (Z, 2)): [(QUERY, XB)],
    (O_ALL, X): [(QUERY, XB)],
    (W_Z, (2, 1)): [KV_ACT_X],
    (COT, (Z, 1)): [KV_ACT_X],
    (W_X, (2, 0)): [BRANCH_Y],
    BRANCH_C: [(W_Z, (2, 1)), (COT, (Z, 1))],
    (W_Z, (2, 2)): [ATTENDED],
    (W_Z, (1, 0)): [ATTENDED],
    (W_X, (2, 1)): [(W_X, (2, 0))],
    (COT, YA): [ATTENDED],
    NORMED_TWO: [(W_Z, (2, 2)), (W_X, (0, 0)), (COT, YA)],
    (W_X, (2, 2)): [(W_X, (2, 1))],
    (COT, YB): [BRANCH_Y],
    (N2, (Z, 1)): [(W_Z, (1, 0)), (W_X, (2, 1)), (COT, YB)],
    (W_Z, (3, 0)): [(N2, (Z, 2))],
    (W_X, (1, 0)): [(N2, (Z, 2))],
    (N2, YB): [(W_Z, (3, 0))],
    (W_Z, (3, 1)): [(N2, (Z, 1))],
    (W_X, (3, 0)): [(W_X, (1, 0))],
    (COT, C): [(N2, (Z, 1))],
    (N2, C): [(W_Z, (3, 1)), (W_X, (1, 0))],
    (W_Z, (3, 2)): [(N2, YB)],
    (W_X, (3, 1)): [(W_X, (3, 0))],
    (W_X, (3, 2)): [(W_X, (3, 1))],
    INPUTS: [(QUERY, (Z, 2))],
    POSITIONS: [(QUERY, (Z, 2))],
    MASK: [(QUERY, (Z, 1))],
    W_PREP: [(KV, C)],
    GRADS_FAR: [(DN, OWN)],
    (DN, (Z, 1)): [GRADS_FAR],
    GRADS_NEAR: [(DN, YB)],
    (DN, (Z, 2)): [GRADS_NEAR],
    (G_X, 2): [(G_X, 3)],
    (DRES, Y): [(G_X, 3)],
    (FFN, AWAY): [(DN, (Z, 2))],
    (FFN, OWN): [(DN, (Z, 2))],
    (DRES, C): [(FFN, OWN), (FFN, AWAY)],
    (G_Z, 3): [(DN, (Z, 2))],
    (G_X, 1): [(G_X, 2)],
    KV_GRAD_C: [(G_X, 2)],
    (FFN, C): [(DRES, C)],
    KV_GRAD_X: [(FFN, C)],
    (PROJ, XF): [(G_X, 1), (G_Z, 3)],
    (FFN, Y): [KV_GRAD_C],
    (DN1, C): [(PROJ, GRAD)],
    (G_Z, 2): [(G_Z, 3)],
    (G_Z, 1): [KV_GRAD_X],
    (PROJ, (Z, 1)): [(FFN, Y), (G_Z, 1)],
    (PROJ, (Z, 2)): [(DN1, Y), (FFN, (Z, 1))],
    (VECTOR, C): [(PROJ, XN)],
    (OUT, X): [(PROJ, XN)],
    (FFN, (Z, 1)): [(FFN, Y)],
    (G_X, 0): [(OUT, X)],
    (OUT, GRAD): [KV_GRAD_C],
    KV_DONE_Y: [(G_Z, 2)],
    HEADS: [(W_Z, (2, 0))],
}


def after(x, *tokens):
    return lax.optimization_barrier((x, *tokens))[0] if tokens else x


def index(x, i, axis=0):
    return lax.dynamic_index_in_dim(x, i, axis, keepdims=False)


def split_columns(weights, n, pieces):
    rows, columns = weights[0].shape
    part, count = columns // n, len(weights)
    flat = [(j, cut) for j in range(n) for cut in pieces[j]]

    def kernel(*refs):
        ins, outs, held = refs[:count], refs[count:-1], refs[-1]
        d = lax.axis_index("dp")
        for i in range(count):
            for t in range(n):
                held[t] = ins[i][:, t * part : (t + 1) * part]
            for out, (j, (low, high)) in zip(outs, flat):
                out[i] = held[d ^ j, low:high]

    outs = pl.pallas_call(
        kernel,
        cost_estimate=CHEAP,
        out_shape=[
            jax.ShapeDtypeStruct((count, high - low, part), BF) for _, (low, high) in flat
        ],
        scratch_shapes=[pltpu.VMEM((n, rows, part), BF)],
        compiler_params=pltpu.CompilerParams(vmem_limit_bytes=48 << 20),
    )(*weights)
    return dict(zip(flat, outs))


def join_columns(blocks):
    n = len(blocks)
    count, rows, part = blocks[0].shape

    def kernel(*refs):
        ins, outs, held = refs[:n], refs[n:-1], refs[-1]
        d = lax.axis_index("dp")
        for i in range(count):
            for j, ref in enumerate(ins):
                held[d ^ j] = ref[i]
            for t in range(n):
                outs[i][:, t * part : (t + 1) * part] = held[t].astype(F32)

    return pl.pallas_call(
        kernel,
        cost_estimate=CHEAP,
        out_shape=[jax.ShapeDtypeStruct((rows, n * part), F32)] * count,
        scratch_shapes=[pltpu.VMEM((n, rows, part), BF)],
        compiler_params=pltpu.CompilerParams(vmem_limit_bytes=48 << 20),
    )(*blocks)


def key_value_slots(w_key, w_value, vectors):
    rows = w_key.shape[0]

    def kernel(key_ref, value_ref, *refs):
        ins, outs = refs[:-2], refs[-2:]
        head = lax.axis_index("mp") // (lax.axis_size("mp") // KVH)
        for i, ref in enumerate((key_ref, value_ref)):
            parts = [ref[:, k * HD : (k + 1) * HD] for k in range(KVH)]
            outs[0][i, :rows] = jnp.where(head == 0, parts[0], parts[1])
            outs[1][i, :rows] = jnp.where(head == 0, parts[1], parts[0])
            for out in outs:
                out[i, rows:] = jnp.zeros((SMALL, HD), BF)
                for j, vector in enumerate(ins):
                    out[i, rows + j : rows + j + 1, : vector.shape[1]] = vector[...]

    return pl.pallas_call(
        kernel, cost_estimate=CHEAP, out_shape=[jax.ShapeDtypeStruct((2, rows + SMALL, HD), BF)] * 2
    )(w_key, w_value, *[v[None] for v in vectors])


def join_rows(own, other, n_dp, n_seq, rows, lens):
    parts = [(a, o, 0) for a, o in own] + [(a, o, 1) for a, o in other]
    width = parts[0][0].shape[2]
    total = sum(len(o) for _, o, _ in parts)
    slots = n_dp * n_seq
    small = parts[0][0].shape[1] - rows

    def kernel(*refs):
        ins, out, vectors = refs[: len(parts)], refs[len(parts)], refs[len(parts) + 1 : -2]
        held, sem = refs[-2:]
        d = lax.axis_index("dp")
        s = lax.axis_index("seq")
        copies = []
        for ref, (_, offsets, side) in zip(ins, parts):
            for i, offset in enumerate(offsets):
                slot = (d ^ offset) * n_seq + (s ^ side)
                start = pl.multiple_of(slot * rows, rows)
                pairs = [(ref.at[i, pl.ds(0, rows)], out.at[pl.ds(start, rows)])]
                if lens:
                    pairs.append((ref.at[i, pl.ds(rows, small)], held.at[slot]))
                for pair in pairs:
                    copies.append(pltpu.make_async_copy(*pair, sem.at[len(copies)]))
        for copy in copies:
            copy.start()
        for copy in copies:
            copy.wait()
        for i, size in enumerate(lens):
            for t in range(slots):
                for k in range(small // SMALL):
                    at = (t * (small // SMALL) + k) * size
                    x = held[t, k * SMALL : (k + 1) * SMALL, :size].astype(F32)
                    vectors[i][:, at : at + size] = x[i : i + 1]

    return pl.pallas_call(
        kernel,
        cost_estimate=CHEAP,
        out_shape=[jax.ShapeDtypeStruct((slots * rows, width), BF)]
        + [jax.ShapeDtypeStruct((1, slots * (small // SMALL) * size), F32) for size in lens],
        in_specs=[pl.BlockSpec(memory_space=pl.ANY)] * len(parts),
        scratch_shapes=[
            pltpu.VMEM((slots, max(small, SMALL), width), BF),
            pltpu.SemaphoreType.DMA((2 * total,)),
        ],
    )(*[a for a, _, _ in parts])


def turn(x, cosine, sine_signed):
    return x * cosine + pltpu.roll(x, HD // 2, 1) * sine_signed


def project(x, vectors, w_q, w_kv, cosine, sine_signed):
    tokens = x.shape[0]
    wide = w_q.shape[1]

    def kernel(x_ref, bq, bk, bv, gain, _, w_ref, wkv_ref, cos_ref, sin_ref, *outs):
        normed, inv_ref, q_ref, kv_ref = outs
        m = lax.axis_index("mp")
        value = x_ref[...].astype(F32)
        inv = inverse_rms(value)
        inv_ref[...] = inv
        norm = (value * inv * gain[...]).astype(BF)
        normed[...] = norm
        proj = dot(norm, w_ref[...])
        cosine, sine = cos_ref[...], sin_ref[...]
        bias = bq[:, pl.ds(pl.multiple_of(m * wide, HD), wide)]
        for j in range(wide // HD):
            cut = slice(j * HD, (j + 1) * HD)
            q_ref[:, cut] = turn(proj[:, cut] + bias[:, cut], cosine, sine).astype(BF)
        head = pl.ds(pl.multiple_of((m // 2) * HD, HD), HD)
        last = dot(norm, wkv_ref[...]) + jnp.where(m % 2 == 0, bk[:, head], bv[:, head])
        kv_ref[...] = jnp.where(m % 2 == 0, turn(last, cosine, sine), last).astype(BF)

    return pl.pallas_call(
        kernel,
        cost_estimate=CHEAP,
        out_shape=[
            jax.ShapeDtypeStruct(x.shape, BF),
            jax.ShapeDtypeStruct((tokens, 1), F32),
            jax.ShapeDtypeStruct((tokens, wide), BF),
            jax.ShapeDtypeStruct((tokens, HD), BF),
        ],
    )(x, *vectors, w_q, w_kv, cosine, sine_signed)


def attend(query, seen, other, mask, out_t, quarter):
    tokens, wide = query.shape
    heads = wide // HD
    width = out_t.shape[0]

    def kernel(q_ref, seen_ref, other_ref, mask_ref, o_ref, att, log_ref, near, away, held):
        c = lax.axis_index("mp") % 2
        keys = jnp.where(c == 0, seen_ref[...], other_ref[...])
        vals = jnp.where(c == 0, other_ref[...], seen_ref[...])
        for j in range(heads):
            cut = slice(j * HD, (j + 1) * HD)
            scores = dot_nt(q_ref[:, cut], keys) * HD ** (-0.5) + mask_ref[...]
            top = jnp.max(scores, axis=-1, keepdims=True)
            total = jnp.sum(jnp.exp(scores - top), axis=-1, keepdims=True)
            log_total = top + jnp.log(total)
            log_ref[:, j : j + 1] = log_total
            att[:, cut] = dot(jnp.exp(scores - log_total).astype(BF), vals).astype(BF)
        held[...] = dot_nt(att[...], o_ref[...])
        for i in range(2):
            rows = pl.ds(pl.multiple_of((2 * i + c) * quarter, quarter), quarter)
            near[i] = held[rows]
            rows = pl.ds(pl.multiple_of((2 * i + 1 - c) * quarter, quarter), quarter)
            away[i] = held[rows].astype(BF)

    return pl.pallas_call(
        kernel,
        cost_estimate=CHEAP,
        out_shape=[
            jax.ShapeDtypeStruct((tokens, wide), BF),
            jax.ShapeDtypeStruct((tokens, heads), F32),
            jax.ShapeDtypeStruct((2, quarter, width), F32),
            jax.ShapeDtypeStruct((2, quarter, width), BF),
        ],
        scratch_shapes=[pltpu.VMEM((tokens, width), F32)],
    )(query, seen, other, mask, out_t)


def feed_rows(n2, cot, gate_ref, up_ref, down_ref, outs, waits):
    act, diff_gate_ref, diff_up_ref, dn = outs
    size = min(256, n2.shape[0])
    for i in range(n2.shape[0] // size):
        rows = slice(i * size, (i + 1) * size)
        if i == 0:
            waits[0]()
        gate_proj = dot(n2[rows], gate_ref[...])
        if i == 0:
            waits[1]()
        up_proj = dot(n2[rows], up_ref[...])
        if i == 0:
            waits[2]()
        diff_hidden = dot(cot[rows], down_ref[...])
        sigmoid_gate = 1.0 / (1.0 + jnp.exp(-gate_proj))
        silu_gate = gate_proj * sigmoid_gate
        act[rows] = (silu_gate * up_proj).astype(BF)
        diff_gate = (
            diff_hidden * up_proj * sigmoid_gate * (1.0 + gate_proj * (1.0 - sigmoid_gate))
        ).astype(BF)
        diff_up = (diff_hidden * silu_gate).astype(BF)
        diff_gate_ref[rows] = diff_gate
        diff_up_ref[rows] = diff_up
        dn[rows] = (dot_nt(diff_gate, gate_ref[...]) + dot_nt(diff_up, up_ref[...])).astype(dn.dtype)


def feed_shapes(n2, part, kind):
    shape = jax.ShapeDtypeStruct((n2.shape[0], part), BF)
    return [shape] * 3 + [jax.ShapeDtypeStruct(n2.shape, kind)]


def feed_limit(n2, part):
    part = -(-part // HD) * HD
    return min(60 << 20, (10 << 20) + 8 * n2.size + 12 * sum(n2.shape) * part)


def feed_first(n2, cot, blocks, rows, n_dp, n_seq):
    keys = list(blocks)
    part = blocks[keys[0]].shape[2]
    full = n_dp * n_seq * rows

    def kernel(n2_ref, cot_ref, *refs):
        ins, copies_out, outs = refs[: len(keys)], refs[len(keys) :][:3], refs[len(keys) + 3 :][:4]
        weights, sem = refs[-4:-1], refs[-1]
        d = lax.axis_index("dp")
        s = lax.axis_index("seq")
        back = [
            pltpu.make_async_copy(weights[w], copies_out[w], sem.at[w]) for w in range(3)
        ]

        def place(which):
            for ref, (side, j, (low, high)) in zip(ins, keys):
                size = high - low
                start = ((d ^ j) * n_seq + (s ^ side)) * rows + low
                weights[which][pl.ds(pl.multiple_of(start, size), size)] = ref[which]
            back[which].start()

        waits = [lambda w=w: place(w) for w in range(3)]
        feed_rows(n2_ref, cot_ref, *weights, outs, waits)
        for copy in back:
            copy.wait()

    whole = pl.BlockSpec(memory_space=pltpu.VMEM)
    return pl.pallas_call(
        kernel,
        cost_estimate=CHEAP,
        out_shape=[pltpu.HBM((full, part), BF)] * 3 + feed_shapes(n2, part, BF),
        out_specs=[pl.BlockSpec(memory_space=pltpu.HBM)] * 3 + [whole] * 4,
        scratch_shapes=[pltpu.VMEM((full, part), BF)] * 3
        + [pltpu.SemaphoreType.DMA((3,))],
        compiler_params=pltpu.CompilerParams(vmem_limit_bytes=feed_limit(n2, part)),
    )(n2, cot, *blocks.values())


def feed_second(n2, cot, gate, up, down):
    part = gate.shape[1]

    def kernel(n2_ref, cot_ref, gate_ref, up_ref, down_ref, *outs):
        feed_rows(n2_ref, cot_ref, gate_ref, up_ref, down_ref, outs, [lambda: None] * 3)

    return pl.pallas_call(
        kernel,
        cost_estimate=CHEAP,
        out_shape=feed_shapes(n2, part, F32),
        compiler_params=pltpu.CompilerParams(vmem_limit_bytes=feed_limit(n2, part)),
    )(n2, cot, gate, up, down)


def weight_grads(rows, which, diffs, n_dp, n_seq, far):
    count, half, n = len(diffs), n_dp // 2, 2 * len(rows)
    wide = rows[0][0].shape[1] // n_dp
    size, width = wide // n_seq, diffs[0][0].shape[1]
    operands = [a for pair in rows for a in pair] + [a for pair in diffs for a in pair]

    def kernel(*refs):
        ins, outs, held = refs[: len(operands)], refs[len(operands) : -1], refs[-1]
        d = lax.axis_index("dp")
        s = lax.axis_index("seq")
        upper = (d // half) ^ int(far)

        def columns(ref, t):
            if wide % HD == 0:
                start = upper * (half * wide) + t * wide
                return ref[:, pl.ds(pl.multiple_of(start, HD), wide)]
            low = ref[:, t * wide : (t + 1) * wide]
            high = ref[:, (half + t) * wide : (half + t + 1) * wide]
            return jnp.where(upper == 0, low, high)

        for i in range(count):
            for t in range(half):
                k = 2 * which[i]
                x = dot_tn(columns(ins[k], t), ins[n + 2 * i][...])
                x = x + dot_tn(columns(ins[k + 1], t), ins[n + 2 * i + 1][...])
                x = x.astype(BF)
                held[t, 0] = x[:size]
                held[t, 1] = x[size:]
            for j in range(half):
                outs[j][i] = held[(d % half) ^ j, s]
                outs[half + j][i] = held[(d % half) ^ j, 1 - s]

    total = sum(a.size for a in operands)
    need = (6 << 20) + (2 if total < 8 << 20 else 4) * total
    outs = pl.pallas_call(
        kernel,
        cost_estimate=CHEAP,
        out_shape=[jax.ShapeDtypeStruct((count, size, width), BF)] * n_dp,
        scratch_shapes=[pltpu.VMEM((half, n_seq, size, width), BF)],
        compiler_params=pltpu.CompilerParams(vmem_limit_bytes=min(60 << 20, need)),
    )(*operands)
    return outs[:half], outs[half:]


def token_grads(rows, diff, n_dp, n_seq, groups):
    wide = rows.shape[1] // n_dp
    size, width = wide // n_seq, diff.shape[1]

    def kernel(rows_ref, diff_ref, *refs):
        outs, held = refs[:-1], refs[-1]
        d = lax.axis_index("dp")
        s = lax.axis_index("seq")
        for t in range(n_dp):
            x = dot_tn(rows_ref[:, t * wide : (t + 1) * wide], diff_ref[...]).astype(BF)
            held[t, 0] = x[:size]
            held[t, 1] = x[size:]
        for side in range(2):
            for out, group in zip(outs[side * len(groups) :], groups):
                for i, offset in enumerate(group):
                    out[i] = held[d ^ offset, s ^ side]

    outs = pl.pallas_call(
        kernel,
        cost_estimate=CHEAP,
        out_shape=[jax.ShapeDtypeStruct((len(g), size, width), BF) for g in groups] * 2,
        scratch_shapes=[pltpu.VMEM((n_dp, n_seq, size, width), BF)],
    )(rows, diff)
    return outs[: len(groups)], outs[len(groups) :]


def solution(mesh):
    n_dp = mesh.shape["dp"]
    n_seq = mesh.shape["seq"]
    n_mp = mesh.shape["mp"]
    bits = [1 << i for i in reversed(range(n_dp.bit_length() - 1))]

    def on_device(
        inputs,
        cotangent,
        segments,
        positions,
        w_query,
        w_key,
        w_value,
        bias_query,
        bias_key,
        bias_value,
        w_out,
        gain_attn,
        gain_ffn,
        w_gate,
        w_up,
        w_down,
    ):
        d = lax.axis_index("dp")
        s = lax.axis_index("seq")
        m = lax.axis_index("mp")
        y, c = m // 2, m % 2
        tokens = inputs.shape[0]
        quarter = tokens // n_mp
        score_scale = HD ** (-0.5)
        wide = w_query.shape[1]
        heads_local = wide // HD
        rows_kv = w_key.shape[0]

        values, makers = {}, {}

        def get(name):
            if name not in values:
                values[name] = makers[name]()
            return values[name]

        def task(name):
            def add(maker):
                makers[name] = maker

            return add

        def tied(name, x):
            tokens = [jax.tree.leaves(get(o))[0] for o in AFTER.get(name, ()) if o in makers]
            return after(x, *tokens)

        links = {X: ("seq", [(0, 1), (1, 0)]), X01: ("seq", [(0, 1)]), X10: ("seq", [(1, 0)])}
        for k in range(1, n_dp):
            links[(Z, k)] = ("dp", [(j, j ^ k) for j in range(n_dp)])
        for k, name in ((1, C), (2, Y)):
            links[name] = ("mp", [(j, j ^ k) for j in range(n_mp)])

        def move(name, link, maker):
            makers[name] = lambda: lax.ppermute(tied(name, maker()), *links[link])

        def of(name):
            return lambda: get(name)

        def gather(name, maker, size, lens, split):
            makers[(name, PAY)] = lambda: maker()[None]
            pay, offsets = (name, PAY), [0]
            for k in bits[:-1]:
                recv = (name, (Z, k))
                move(recv, (Z, k), of(pay))
                makers[(recv, PAY)] = lambda a=pay, b=recv: jnp.concatenate([get(a), get(b)])
                pay, offsets = (recv, PAY), offsets + [o ^ k for o in offsets]
            k = bits[-1]
            recv = (name, (Z, k))
            move(recv, (Z, k), of(pay))
            there = [o ^ k for o in offsets]
            if split:
                move((name, XA), X, of(pay))
                move((name, XB), X, of(recv))
                own = lambda: [(get(pay), offsets), (get(recv), there)]
                other = lambda: [(get((name, XA)), offsets), (get((name, XB)), there)]
            else:
                makers[(name, BOTH)] = lambda: jnp.concatenate([get(pay), get(recv)])
                move((name, X), X, of((name, BOTH)))
                own = lambda: [(get((name, BOTH)), offsets + there)]
                other = lambda: [(get((name, X)), offsets + there)]
            makers[name] = lambda: join_rows(own(), other(), n_dp, n_seq, size, lens)

        w_rows = w_gate.shape[0]
        whole_cut = [(0, w_rows)]
        third = w_rows // 3
        third_cuts = [(i * third, (i + 1) * third) for i in range(3)]
        pieces = [whole_cut if k < n_dp // 2 else third_cuts for k in range(n_dp)]
        tails = [(k, cut, (k, i)) for k in range(n_dp) for i, cut in enumerate(pieces[k])]
        makers[W_PREP] = lambda: split_columns(
            [tied(W_PREP, w_gate), w_up, w_down.T], n_dp, pieces
        )
        for k, cut, tail in tails:
            if k:
                move((W_Z, tail), (Z, k), lambda k=k, cut=cut: get(W_PREP)[k, cut])
            else:
                makers[(W_Z, tail)] = lambda cut=cut: get(W_PREP)[0, cut]
            move((W_X, tail), X, of((W_Z, tail)))

        def rows_gather(name, maker):
            makers[(name, PAY)] = maker
            pay = (name, PAY)
            for k in bits[:-1]:
                recv = (name, (Z, k))
                move(recv, (Z, k), of(pay))
                makers[(recv, PAY)] = lambda a=pay, b=recv: jnp.concatenate([get(a), get(b)])
                pay = (recv, PAY)
            recv = (name, (Z, bits[-1]))
            move(recv, (Z, bits[-1]), of(pay))
            move((name, YA), Y, of(pay))
            move((name, YB), Y, of(recv))
            makers[(name, OWN)] = lambda: jnp.concatenate(
                [get(pay), get(recv), get((name, YA)), get((name, YB))]
            )
            move((name, C), C, of((name, OWN)))

        def rows_sum(name, split):
            move((name, C), C, of((name, AWAY)))
            last = (name, (Z, bits[-1]))

            def part(i):
                size = get((name, OWN)).shape[0] // 4
                cut = slice(i * size, (i + 1) * size)
                return get((name, OWN))[cut] + get((name, C))[cut].astype(F32)

            for i in range(4):
                makers[(name, PART, i)] = lambda i=i: part(i)
            if split:
                move((name, YB), Y, lambda: get((name, PART, 3)).astype(BF))
                move((name, YA), Y, lambda: get((name, PART, 2)).astype(BF))
            else:

                def parts():
                    return jnp.concatenate([get((name, PART, 2)), get((name, PART, 3))]).astype(BF)

                move((name, Y), Y, parts)
                makers[(name, YA)] = lambda: get((name, Y))[: get((name, PART, 2)).shape[0]]
                makers[(name, YB)] = lambda: get((name, Y))[get((name, PART, 2)).shape[0] :]
            move(
                last,
                (Z, bits[-1]),
                lambda: (get((name, PART, 1)) + get((name, YB)).astype(F32)).astype(BF),
            )
            makers[(name, LEFT, 0)] = (
                lambda: get((name, PART, 0)) + get((name, YA)).astype(F32) + get(last).astype(F32)
            )
            left = (name, LEFT, 0)
            for i, k in enumerate(reversed(bits[:-1])):
                recv = (name, (Z, k))

                def far(left=left):
                    return get(left)[get(left).shape[0] // 2 :].astype(BF)

                def near(left=left, recv=recv):
                    return get(left)[: get(left).shape[0] // 2] + get(recv).astype(F32)

                move(recv, (Z, k), far)
                left = (name, LEFT, i + 1)
                makers[left] = near
            makers[name] = of(left)

        def weight_grad_ways(name, far):
            own, away = get(HIDDEN_OWN), get(HIDDEN_AWAY)
            n2 = [tied(name, get((N2, OWN))), get((N2, C))]
            cot = [get((COT, OWN)), get((COT, C))]
            return weight_grads(
                [n2, cot],
                [0, 0, 1],
                [[own[1], away[1]], [own[2], away[2]], [own[0], away[0]]],
                n_dp,
                n_seq,
                far,
            )

        makers[GRADS_FAR] = lambda: weight_grad_ways(GRADS_FAR, True)
        makers[GRADS_NEAR] = lambda: weight_grad_ways(GRADS_NEAR, False)

        def grad_piece(k, side):
            return get(GRADS_NEAR if k < n_dp // 2 else GRADS_FAR)[side][k % (n_dp // 2)]

        for k in range(n_dp):
            move((G_X, k), X, lambda k=k: grad_piece(k, 1))
        for k in range(n_dp):

            def summed(k=k):
                own = tied((G_SUM, k), grad_piece(k, 0)).astype(F32)
                return (own + get((G_X, k)).astype(F32)).astype(BF)

            makers[(G_SUM, k)] = summed
            if k:
                move((G_Z, k), (Z, k), of((G_SUM, k)))
            else:
                makers[(G_Z, k)] = of((G_SUM, k))
        makers[GRADS_DONE] = lambda: join_columns(
            [get((G_Z, k)) for k in range(n_dp)]
        )

        def gather_grad(name, rows, diff, split):
            near = [0]
            for k in bits[:-1]:
                near = near + [o ^ k for o in near]
            far = [o ^ bits[-1] for o in near]
            n_near = len(near)
            groups = [near, far] if split else [near + far]
            makers[(name, GRAD)] = lambda: token_grads(rows(), diff(), n_dp, n_seq, groups)
            if split:
                move((name, XF), X, lambda: get((name, GRAD))[1][1])
                move((name, XN), X, lambda: get((name, GRAD))[1][0])
                own = lambda i: get((name, GRAD))[0][i]
            else:
                move((name, X), X, lambda: get((name, GRAD))[1][0])
                makers[(name, XN)] = lambda: get((name, X))[:n_near]
                makers[(name, XF)] = lambda: get((name, X))[n_near:]
                own = lambda i: get((name, GRAD))[0][0][i * n_near : (i + 1) * n_near]

            def both(i, recv):
                return own(i).astype(F32) + get(recv).astype(F32)

            last = (name, (Z, bits[-1]))
            move(last, (Z, bits[-1]), lambda: both(1, (name, XF)).astype(BF))
            makers[(name, LEFT, 0)] = lambda: both(0, (name, XN)) + get(last).astype(F32)
            left = (name, LEFT, 0)
            for i, k in enumerate(reversed(bits[:-1])):
                recv = (name, (Z, k))

                def far_half(left=left):
                    return get(left)[get(left).shape[0] // 2 :].astype(BF)

                def near_half(left=left, recv=recv):
                    return get(left)[: get(left).shape[0] // 2] + get(recv).astype(F32)

                move(recv, (Z, k), far_half)
                left = (name, LEFT, i + 1)
                makers[left] = near_half
            makers[(name, DONE)] = lambda: get(left)[0]

        def mp_gather(name, maker):
            move((name, Y), Y, maker)

            def pair():
                a, b = maker(), get((name, Y))
                return jnp.where(y == 0, jnp.stack([a, b]), jnp.stack([b, a]))

            makers[(name, PAIR)] = pair
            move((name, C), C, of((name, PAIR)))

            def whole():
                a, b = get((name, PAIR)), get((name, C))
                both = jnp.where(c == 0, jnp.stack([a, b], axis=1), jnp.stack([b, a], axis=1))
                return both.reshape(-1, both.shape[-1])

            makers[name] = whole

        def mp_sum(name, maker):
            def blocks():
                x = maker()
                return x.reshape(2, 2, -1, x.shape[-1])

            makers[(name, BLOCKS)] = blocks
            move((name, C), C, lambda: index(get((name, BLOCKS)), 1 - c, 1).astype(BF))
            makers[(name, HALF)] = lambda: index(get((name, BLOCKS)), c, 1) + get(
                (name, C)
            ).astype(F32)
            move((name, Y), Y, lambda: index(get((name, HALF)), 1 - y).astype(BF))
            makers[name] = lambda: index(get((name, HALF)), y) + get((name, Y)).astype(F32)

        gather(QUERY, lambda: w_query, w_query.shape[0], [], True)
        gather(O_ALL, lambda: tied(O_ALL, w_out).T, w_query.shape[0], [], False)
        makers[OUT_FULL] = lambda: get(O_ALL)[0]

        vectors = (bias_query, bias_key, bias_value, gain_attn, gain_ffn)

        makers[KV_SLOTS] = lambda: key_value_slots(w_key, w_value, vectors)
        move((KV, Y), Y, lambda: get(KV_SLOTS)[1])

        @task(KV_PAIRS)
        def kv_pairs():
            return jnp.stack([get(KV_SLOTS)[0], get((KV, Y))])

        move((KV, C), C, lambda: index(get(KV_PAIRS), 1 - c, 1))

        @task(KV_ROWS)
        def kv_rows():
            own, got = index(get(KV_PAIRS), c, 1), get((KV, C))
            by_core = jnp.where(
                c == 0, jnp.stack([own, got], axis=1), jnp.stack([got, own], axis=1)
            )
            whole = jnp.where(y == 0, by_core, by_core[::-1])
            parts = [whole[:, :, :rows_kv], whole[:, :, rows_kv:]]
            return jnp.concatenate([x.reshape(-1, HD) for x in parts])

        gather(
            KV, of(KV_ROWS), n_mp * rows_kv, [v.shape[0] for v in vectors], False
        )

        @task(IN_FLOAT)
        def in_float():
            return tied(INPUTS, inputs).astype(F32)

        @task(ROPE)
        def rope():
            cosine, sine_table = rope_tables(tied(POSITIONS, positions))
            first = jnp.arange(HD) < HD // 2
            return cosine, jnp.where(first, -sine_table, sine_table)

        @task(PROJECTED)
        def projected():
            weights, *small = get(KV)
            x = tied(PROJECT, inputs)
            return project(x, small, get(QUERY)[0], weights, *get(ROPE))

        makers[NORMED_ONE] = lambda: get(PROJECTED)[0]
        makers[INV_ONE] = lambda: get(PROJECTED)[1]
        makers[QUERY_ROT] = lambda: get(PROJECTED)[2]
        makers[KV_ROT] = lambda: tied(KV_ROT, get(PROJECTED)[3])

        move(KV_ACT_X, X01, of(KV_ROT))

        @task(KV_SEEN)
        def kv_seen():
            return jnp.concatenate([get(KV_ACT_X), get(KV_ROT)], axis=0)

        move(KV_ACT_C, C, of(KV_SEEN))

        @task(MASK_TABLE)
        def mask_table():
            where = tied(MASK, segments)
            seg_before = where[:tokens]
            seg_own = lax.dynamic_slice_in_dim(where, s * tokens, tokens, 0)
            order = jnp.arange(tokens, dtype=jnp.int32)
            before = (seg_own[:, None] == seg_before[None, :]) & (s > 0)
            own = (seg_own[:, None] == seg_own[None, :]) & (order[None, :] <= order[:, None])
            return jnp.where(jnp.concatenate([before, own], axis=1), 0.0, NEG_BIG)

        @task(HEADS)
        def heads():
            return attend(
                get(QUERY_ROT),
                get(KV_SEEN),
                tied(HEADS, get(KV_ACT_C)),
                get(MASK_TABLE),
                get(OUT_FULL),
                quarter,
            )

        makers[ATTENDED] = lambda: get(HEADS)[0]

        move(BRANCH_C, C, lambda: get(HEADS)[3])
        makers[BRANCH_HALF] = lambda: get(HEADS)[2] + get(BRANCH_C).astype(F32)
        move(BRANCH_Y, Y, lambda: index(get(BRANCH_HALF), 1 - y).astype(BF))
        makers[BRANCH] = lambda: index(get(BRANCH_HALF), y) + get(BRANCH_Y).astype(F32)

        @task(IN_QUARTER)
        def in_quarter():
            return lax.dynamic_slice_in_dim(get(IN_FLOAT), m * quarter, quarter, 0)

        @task(HIDDEN_RES)
        def hidden_res():
            return get(IN_QUARTER) + get(BRANCH)

        @task(INV_TWO)
        def inv_two():
            return inverse_rms(get(HIDDEN_RES))

        @task(NORMED_TWO)
        def normed_two():
            return tied(
                NORMED_TWO, (get(HIDDEN_RES) * get(INV_TWO) * get(KV)[5]).astype(BF)
            )

        @task(COT_QUARTER)
        def cot_quarter():
            return lax.dynamic_slice_in_dim(cotangent, m * quarter, quarter, 0)

        rows_gather(N2, of(NORMED_TWO))
        rows_gather(COT, of(COT_QUARTER))

        @task(FEED_AWAY)
        def feed_away():
            blocks = {(0, k, cut): get((W_Z, tail)) for k, cut, tail in tails}
            blocks.update({(1, k, cut): get((W_X, tail)) for k, cut, tail in tails})
            return feed_first(
                tied(FEED_AWAY, get((N2, C))), get((COT, C)), blocks, w_rows, n_dp, n_seq
            )

        @task(FEED_OWN)
        def feed_own():
            weights = get(FEED_AWAY)[:3]
            return feed_second(tied(FEED_OWN, get((N2, OWN))), get((COT, OWN)), *weights)

        makers[HIDDEN_AWAY] = lambda: get(FEED_AWAY)[3:6]
        makers[HIDDEN_OWN] = lambda: get(FEED_OWN)[:3]
        makers[(DN, AWAY)] = lambda: get(FEED_AWAY)[6]
        makers[(DN, OWN)] = lambda: get(FEED_OWN)[3]
        makers[(FFN, OWN)] = lambda: dot_nt(
            tied((FFN, OWN), get(HIDDEN_OWN)[0]), get(FEED_AWAY)[2]
        )
        makers[(FFN, AWAY)] = lambda: dot_nt(
            tied((FFN, AWAY), get(HIDDEN_AWAY)[0]), get(FEED_AWAY)[2]
        ).astype(BF)
        rows_sum(DN, True)

        rows_sum(FFN, False)

        @task(DIFF_RES)
        def diff_res():
            return get(COT_QUARTER).astype(F32) + norm_backward(
                get(DN), get(HIDDEN_RES), get(INV_TWO), get(KV)[5]
            )

        mp_gather(DRES, lambda: get(DIFF_RES).astype(BF))

        @task(HEADS_BACK)
        def heads_back():
            seen, other = get(KV_SEEN), get(KV_ACT_C)
            keys, vals = jnp.where(c == 0, seen, other), jnp.where(c == 0, other, seen)
            queries, logs = get(QUERY_ROT), get(HEADS)[1]
            diff_attended = tied(HEADS_BACK, dot(get(DRES), get(OUT_FULL)).astype(BF))
            return [
                head_backward(
                    queries[:, j * HD : (j + 1) * HD],
                    keys,
                    vals,
                    get(MASK_TABLE),
                    score_scale,
                    logs[:, j : j + 1],
                    get(ATTENDED)[:, j * HD : (j + 1) * HD],
                    diff_attended[:, j * HD : (j + 1) * HD],
                )
                for j in range(heads_local)
            ]

        @task(KV_SUMS)
        def kv_sums():
            return [sum(head[i] for head in get(HEADS_BACK)) for i in (1, 2)]

        move(KV_GRAD_C, C, lambda: jnp.where(c == 0, *reversed(get(KV_SUMS))))

        @task(KV_SUM)
        def kv_sum():
            return jnp.where(c == 0, *get(KV_SUMS)) + get(KV_GRAD_C)

        move(KV_GRAD_X, X10, lambda: get(KV_SUM)[:tokens])

        def turn_back(x):
            cosine, sine_signed = get(ROPE)
            return x * cosine - jnp.roll(x, HD // 2, axis=1) * sine_signed

        @task(KV_PRE)
        def kv_pre():
            mine = get(KV_SUM)[tokens:] + get(KV_GRAD_X)
            return jnp.where(c == 0, turn_back(mine), mine)

        @task(QUERY_PRE)
        def query_pre():
            return jnp.concatenate([turn_back(head[0]) for head in get(HEADS_BACK)], axis=1)

        @task(QKV_CAST)
        def qkv_cast():
            return jnp.concatenate([get(QUERY_PRE), get(KV_PRE)], axis=1).astype(BF)

        gather_grad(PROJ, of(NORMED_ONE), of(QKV_CAST), True)
        gather_grad(OUT, lambda: tied((OUT, GRAD), get(DRES)), of(ATTENDED), False)

        @task(DIFF_NORMED)
        def diff_normed():
            cast = get(QKV_CAST)
            return dot_nt(cast[:, :wide], get(QUERY)[0]) + dot_nt(cast[:, wide:], get(KV)[0])

        mp_sum(DN1, of(DIFF_NORMED))

        @task((KV, DONE))
        def kv_done():
            return get((PROJ, DONE))[:, wide:].reshape(2, 2, rows_kv, HD).astype(BF)

        move(KV_DONE_Y, Y, lambda: index(get((KV, DONE)), 1 - y))

        @task(KV_DONE_HEADS)
        def kv_done_heads():
            mine, got = index(get((KV, DONE)), y), get(KV_DONE_Y)
            return jnp.where(y == 0, jnp.stack([mine, got]), jnp.stack([got, mine]))

        move(KV_DONE_C, C, lambda: index(get(KV_DONE_HEADS), 1 - c, 1))

        @task(KV_GRADS)
        def kv_grads():
            mine, got = index(get(KV_DONE_HEADS), c, 1), get(KV_DONE_C)
            return [
                jnp.where(c == 0, a, b)
                .transpose(1, 0, 2)
                .reshape(rows_kv, KVH * HD)
                .astype(F32)
                for a, b in ((mine, got), (got, mine))
            ]

        @task(INV_QUARTER)
        def inv_quarter():
            return lax.dynamic_slice_in_dim(get(INV_ONE), m * quarter, quarter, 0)

        @task(INPUT_DIFF)
        def input_diff():
            return get(DIFF_RES) + norm_backward(
                get(DN1), get(IN_QUARTER), get(INV_QUARTER), get(KV)[4]
            )

        mp_gather(
            RESULTS,
            lambda: jnp.concatenate(
                [get(HIDDEN_RES) + get(FFN), get(INPUT_DIFF)], axis=1
            ).astype(BF),
        )

        @task(VECTOR)
        def vector():
            grad_gain_ffn = jnp.sum(get(DN) * get(HIDDEN_RES) * get(INV_TWO), axis=0)
            grad_gain_attn = jnp.sum(get(DN1) * get(IN_QUARTER) * get(INV_QUARTER), axis=0)
            grad_bq = jnp.sum(get(QUERY_PRE), axis=0)
            grad_bkv = jnp.sum(get(KV_PRE), axis=0)
            zeros_kv = jnp.zeros((2, KVH, HD), F32)
            return jnp.concatenate(
                [
                    lax.dynamic_update_slice_in_dim(
                        jnp.zeros((H * HD,), F32), grad_bq, m * wide, 0
                    ),
                    grad_gain_attn,
                    grad_gain_ffn,
                    lax.dynamic_update_slice(zeros_kv, grad_bkv[None, None], (c, y, 0)).reshape(-1),
                ]
            ).reshape(-1, HD)

        total = VECTOR
        for link in [C, Y, X] + [(Z, k) for k in bits]:
            move((VECTOR, link), link, of(total))
            makers[(TOTAL, link)] = lambda a=total, b=(VECTOR, link): get(a) + get(b)
            total = (TOTAL, link)

        makers[SUMS] = lambda: get(total).reshape(-1)
        device = (d * n_seq + s) * n_mp + m

        def own(start, length):
            width = length // (n_dp * n_seq * n_mp)
            return lax.dynamic_slice_in_dim(
                get(SUMS)[start : start + length], device * width, width, 0
            )

        return (
            get(RESULTS)[:, :D].astype(F32),
            get(RESULTS)[:, D:].astype(F32),
            get((PROJ, DONE))[:, :wide],
            get(KV_GRADS)[0],
            get(KV_GRADS)[1],
            own(0, H * HD),
            get(SUMS)[3 * D : 3 * D + KVH * HD],
            own(3 * D + KVH * HD, KVH * HD),
            get((OUT, DONE)).T,
            own(D, D),
            own(2 * D, D),
            get(GRADS_DONE)[0],
            get(GRADS_DONE)[1],
            get(GRADS_DONE)[2].T,
        )

    in_specs = (
        P(("dp", "seq"), None),
        P(("dp", "seq"), None),
        P("dp"),
        P(("dp", "seq")),
        P(("dp", "seq"), "mp"),
        P(("dp", "seq", "mp"), None),
        P(("dp", "seq", "mp"), None),
        P(("dp", "seq", "mp")),
        P(("dp", "seq", "mp")),
        P(("dp", "seq", "mp")),
        P("mp", ("dp", "seq")),
        P(("dp", "seq", "mp")),
        P(("dp", "seq", "mp")),
        P(("dp", "seq"), "mp"),
        P(("dp", "seq"), "mp"),
        P("mp", ("dp", "seq")),
    )
    out_specs = (
        P(("dp", "seq"), None),
        P(("dp", "seq"), None),
        P(("dp", "seq"), "mp"),
        P(("dp", "seq", "mp"), None),
        P(("dp", "seq", "mp"), None),
        P(("dp", "seq", "mp")),
        P(),
        P(("dp", "seq", "mp")),
        P("mp", ("dp", "seq")),
        P(("dp", "seq", "mp")),
        P(("dp", "seq", "mp")),
        P(("dp", "seq"), "mp"),
        P(("dp", "seq"), "mp"),
        P("mp", ("dp", "seq")),
    )
    return jax.shard_map(
        on_device, mesh=mesh, in_specs=in_specs, out_specs=out_specs, check_vma=False
    )
```
